256 devices in a mesh: patch: 128 (over y, z, x), scene: 2 (over core).
Axes of the slice: x: 4, y: 4, z: 8, core: 2. Of those that a mesh axis runs over, the one named last changes fastest.
Arguments:
- query_rows: bfloat16 [131072, 512], P(('scene', 'patch')), parts along dimension 0, may hold values from -6.2 to 6.2
- key_rows: bfloat16 [131072, 512], P(('scene', 'patch')), parts along dimension 0, may hold values from -6.2 to 6.2
- value_rows: bfloat16 [131072, 512], P(('scene', 'patch')), parts along dimension 0, may hold values from -6 to 6
- grad_output: bfloat16 [131072, 512], P(('scene', 'patch')), parts along dimension 0, may hold values from -6 to 6
- neighbours: int32 [2048, 16], P(('scene', 'patch')), parts along dimension 0, may hold values from 0 to 1023, as said below
- owner: int32 [2048], P('scene'), parts along dimension 0, may hold values from 0 to 1023, as said below
Outputs:
- grad_query: bfloat16 [131072, 512], P(('scene', 'patch')), parts along dimension 0
- grad_key: bfloat16 [131072, 512], P(('scene', 'patch')), parts along dimension 0
- grad_value: bfloat16 [131072, 512], P(('scene', 'patch')), parts along dimension 0
The draws below stay inside these ranges and needn't reach their ends.
There are 2 independent parts, one for each index of `scene`. The reference program is written for one: setup_inputs(seed, part) draws one part's arguments, and reference() takes and returns one part's arrays. A program takes and returns all parts, laid end to end along the dimension named above; each array names one. Nothing has to cross between parts.
Inputs may be any that keep to these rules, and one draw needn't show every extreme that they name: `neighbours`: each row names 16 different patch ids; the query's own patch is among them, and every one is held (through owner) by the query's device or one of the two devices beside it along patch. `owner`: A permutation; each patch id is held by a slot of the device of slots id // 8 * 8 to that plus 8 - 1.
All inputs are finite; a program needn't handle non-finite values.
Results may differ from the reference program's by a relative error of at most 0.011.
Values may be sent and summed in bfloat16 or wider, within the bound.
A program may use at most 128 MiB of HBM per device.

```python
import math
import jax
import jax.numpy as jnp
from jax import lax

HEADS = 8
PATCH = 64
NBR = 16
PATCH_DEV = 8
WIDTH = 512
ROWS = 65536
N_PATCH = 128


def owner_table(base_key):
    random_part = jax.random.randint(base_key, (N_PATCH, PATCH_DEV), 0, 1 << 20)
    ranking = random_part * PATCH_DEV + jnp.arange(PATCH_DEV, dtype=jnp.int32)[None, :]
    order = jnp.argsort(ranking, axis=1).astype(jnp.int32)
    first_slot = jnp.arange(N_PATCH, dtype=jnp.int32)[:, None] * PATCH_DEV
    return (first_slot + order).reshape(-1)


def draw_owner(key, part):
    return owner_table(key)


def draw_neighbours(key, part):
    table = owner_table(key)
    key = jax.random.fold_in(key, 11)
    slot_count = PATCH_DEV * N_PATCH
    span = 3 * PATCH_DEV
    inverse = jnp.zeros((slot_count,), jnp.int32).at[table].set(jnp.arange(slot_count, dtype=jnp.int32))
    query_slot = jnp.arange(slot_count, dtype=jnp.int32)[:, None]
    device = query_slot // PATCH_DEV
    candidate = (device - 1) * PATCH_DEV + jnp.arange(span, dtype=jnp.int32)[None, :]
    valid = (candidate >= 0) & (candidate < slot_count)
    random_part = jax.random.randint(key, (slot_count, span), 0, 1 << 16)
    ranking = random_part * span + jnp.arange(span, dtype=jnp.int32)[None, :]
    ranking = jnp.where(candidate == query_slot, 1 << 28, ranking)
    ranking = jnp.where(valid, ranking, -1)
    picked_values, picked = lax.top_k(ranking, NBR)
    chosen = jnp.take_along_axis(candidate, picked, axis=1)
    chosen = jnp.clip(chosen, 0, slot_count - 1)
    return inverse[chosen]


def draw_query_rows(key, part):
    key = jax.random.fold_in(key, 3)
    rows_out = jnp.clip(jax.random.normal(key, (ROWS, WIDTH), jnp.float32), -6.0, 6.0)
    return rows_out.astype(jnp.bfloat16)


def draw_key_rows(key, part):
    key = jax.random.fold_in(key, 5)
    rows_out = jnp.clip(jax.random.normal(key, (ROWS, WIDTH), jnp.float32), -6.0, 6.0)
    return rows_out.astype(jnp.bfloat16)


def shard_levels(stream_key, dims, cuts, least, top_value):
    level, own = 1.0, jax.random.fold_in(stream_key, 6)
    for dim, blocks in cuts:
        steps = jnp.exp(jax.random.uniform(jax.random.fold_in(own, dim), (blocks,), jnp.float32, least / len(cuts), top_value / len(cuts)))
        level = level * jnp.repeat(steps, dims[dim] // blocks).reshape([-1 if axis == dim else 1 for axis in range(len(dims))])
    return level


def centred(rng, shape, deviation, limit, shards=(), held_as=jnp.bfloat16):
    drawn = jax.random.normal(rng, shape, jnp.float32) * deviation
    if len(shards) > 0:
        drawn = shard_levels(rng, shape, shards, -0.22, 0.18) * drawn
    return jnp.clip(drawn, min=-limit, max=limit).astype(held_as)


def setup_inputs(seed: int = 0, part: int = 0) -> dict:
    arg_keys = jax.random.split(jax.random.key(seed), 7)
    part_splits = jax.random.split(jax.random.fold_in(arg_keys[6], part), 7)
    return {
        "query_rows": draw_query_rows(jax.random.fold_in(jax.random.fold_in(arg_keys[6], part), 71), part),
        "key_rows": draw_key_rows(jax.random.fold_in(jax.random.fold_in(arg_keys[6], part), 71), part),
        "value_rows": centred(part_splits[2], (ROWS, WIDTH), 1.0, 6.0, ((0, 128),)),
        "grad_output": centred(part_splits[3], (ROWS, WIDTH), 1.0, 6.0, ((0, 128),)),
        "neighbours": draw_neighbours(jax.random.fold_in(jax.random.fold_in(arg_keys[6], part), 71), part),
        "owner": draw_owner(jax.random.fold_in(jax.random.fold_in(arg_keys[6], part), 71), part),
    }


def reference(query_rows, key_rows, value_rows, grad_output, neighbours, owner):
    slot_count = PATCH_DEV * N_PATCH
    head_size = query_rows.shape[1] // HEADS
    scaling = 1.0 / math.sqrt(head_size)
    key_slots = owner[neighbours].astype(jnp.int32)
    shape_four = (slot_count, PATCH, HEADS, head_size)
    query_four = query_rows.reshape(shape_four)
    key_four = key_rows.reshape(shape_four)
    value_four = value_rows.reshape(shape_four)
    grad_four = grad_output.reshape(shape_four)

    def step(carry, inputs):
        grad_keys, grad_values = carry
        query_block, grad_block, slot_row = inputs
        query_float = query_block.astype(jnp.float32)
        grad_float = grad_block.astype(jnp.float32)
        key_block = key_four[slot_row].reshape(NBR * PATCH, HEADS, head_size).astype(jnp.float32)
        value_block = value_four[slot_row].reshape(NBR * PATCH, HEADS, head_size).astype(jnp.float32)
        scores = jnp.einsum('qhd,khd->hqk', query_float, key_block) * scaling
        peak = lax.optimization_barrier(jnp.max(scores, axis=-1, keepdims=True))
        log_total = peak + jnp.log(lax.optimization_barrier(jnp.sum(jnp.exp(scores - peak), axis=-1, keepdims=True)))
        weights = jnp.exp(scores - log_total)
        weights_low = weights.astype(jnp.bfloat16).astype(jnp.float32)
        output = jnp.einsum('hqk,khd->qhd', weights_low, value_block)
        delta = lax.optimization_barrier(jnp.sum(grad_float * output, axis=-1))
        dweights = jnp.einsum('qhd,khd->hqk', grad_float, value_block)
        dscores = weights * (dweights - jnp.transpose(delta)[:, :, None])
        dscores_low = dscores.astype(jnp.bfloat16).astype(jnp.float32)
        grad_q = jnp.einsum('hqk,khd->qhd', dscores_low, key_block) * scaling
        part_keys = jnp.einsum('hqk,qhd->khd', dscores_low, query_float) * scaling
        part_values = jnp.einsum('hqk,qhd->khd', weights_low, grad_float)
        grad_keys = grad_keys.at[slot_row].add(part_keys.reshape(NBR, PATCH, HEADS, head_size))
        grad_values = grad_values.at[slot_row].add(part_values.reshape(NBR, PATCH, HEADS, head_size))
        return ((grad_keys, grad_values), grad_q.astype(jnp.bfloat16))
    zeros_four = jnp.zeros(shape_four, jnp.float32)
    (grad_keys, grad_values), grad_q = lax.scan(step, (zeros_four, zeros_four), (query_four, grad_four, key_slots))
    total_shape = query_rows.shape
    return (grad_q.reshape(total_shape), grad_keys.reshape(total_shape).astype(jnp.bfloat16), grad_values.reshape(total_shape).astype(jnp.bfloat16))
```

```python
import functools
import math

import jax
import jax.numpy as jnp
from jax import lax
from jax.experimental import pallas as pl
from jax.experimental.pallas import tpu as pltpu
from jax.sharding import PartitionSpec as P

HEADS = 8
MESH = pl.DeviceIdType.MESH
BF16, F32 = jnp.bfloat16, jnp.float32
MASKED = -1e30
ROWS = 512
TILE = 256
PAIRS = 4
CHUNKS = PAIRS * ROWS // TILE
RING = 5
LAG_B, LAG_C, LAG_D = 2, 4, 7
AHEAD = 2


def dot(left, right):
    return lax.dot_general(left, right, (((1,), (0,)), ((), ())), preferred_element_type=F32)


def dot_last(left, right):
    return lax.dot_general(left, right, (((1,), (1,)), ((), ())), preferred_element_type=F32)


def kernel(
    n,
    query, key, value, gout, neighbours, owner,
    grad_query, grad_key, grad_value,
    own_ids, near_ids, k_pair, v_pair, k_turned, q_all, g_all, bias, hot, mask_out, mask_in,
    e_own, d_own, e_near, d_near, part_own, part_out, part_in, final_out, final_in,
    weights, dscores, dq_own, dq_out, dq_in, dq_done, dk_done, dv_done,
    load_sem, bulk_send, bulk_recv, mask_send, mask_recv, part_send, part_recv,
    final_send, final_recv, dq_send, dq_recv, store_sem,
):
    me = lax.axis_index("patch")
    target = (jnp.minimum(me + 1, n - 1), jnp.maximum(me - 1, 0))
    sends = (me < n - 1, me > 0)
    receives = (me > 0, me < n - 1)
    scaling = 1.0 / math.sqrt(64)
    base2 = scaling * math.log2(math.e)

    barrier = pltpu.get_barrier_semaphore()
    for flow in (0, 1):

        @pl.when(sends[flow])
        def _(flow=flow):
            pl.semaphore_signal(
                barrier, inc=1, device_id={"patch": target[flow]}, device_id_type=MESH
            )

    own_copy = pltpu.make_async_copy(owner, own_ids, load_sem.at[4 * PAIRS])
    near_copy = pltpu.make_async_copy(neighbours, near_ids, load_sem.at[4 * PAIRS + 1])
    own_copy.start()
    near_copy.start()

    def load(pair, array):
        lanes = pl.ds(128 * pair, 128)
        middle = pl.ds(ROWS, ROWS)
        source = (key, value, query, gout)[array].at[:, lanes]
        place = (
            k_pair.at[pair],
            v_pair.at[pair],
            q_all.at[pair, middle],
            g_all.at[pair, middle],
        )[array]
        return pltpu.make_async_copy(source, place, load_sem.at[4 * pair + array])

    for pair in range(PAIRS):
        for array in range(4):
            load(pair, array).start()

    own_copy.wait()
    near_copy.wait()
    lane = lax.broadcasted_iota(jnp.int32, (8, 128), 1)
    low_lane = lax.rem(lane, 64)
    first_id = 8 * (me - 1)
    held = [jnp.full((8, 128), -1, jnp.int32) for _ in range(3)]
    for t in range(24):
        number = first_id + t
        valid = (number >= 0) & (number < 8 * n)
        slot = own_ids[jnp.clip(number, 0, 8 * n - 1)] - first_id
        slot = jnp.where(valid, slot, -1000)
        held = [jnp.where(low_lane == slot - 8 * w, number, held[w]) for w in range(3)]
    near = near_ids[...]
    found = [jnp.zeros((8, 128), jnp.bool_) for _ in range(3)]
    for j in range(16):
        column = jnp.broadcast_to(near[:, j : j + 1], (8, 128))
        found = [found[w] | (column == held[w]) for w in range(3)]
    masks = [jnp.where(found[w] | (low_lane >= 8), 0.0, MASKED) for w in range(3)]
    mask_out[0] = masks[2]
    mask_out[1] = masks[0]

    def spread(block, mask):
        for a in range(8):
            rows = pl.ds(ROWS * block + 64 * a, 64)
            bias[rows, :] = jnp.broadcast_to(mask[a : a + 1, :], (64, 128)).astype(BF16)

    spread(1, masks[1])
    row_slot = lax.broadcasted_iota(jnp.int32, (ROWS, 128), 0) // 64
    lane_slot = lax.rem(lax.broadcasted_iota(jnp.int32, (ROWS, 128), 1), 64)
    hot[...] = jnp.where(row_slot == lane_slot, 1.0, 0.0).astype(BF16)

    for flow in (0, 1):

        @pl.when(jnp.logical_not(receives[flow]))
        def _(flow=flow):
            rows = pl.ds(2 * ROWS * flow, ROWS)
            for pair in range(PAIRS):
                q_all[pair, rows, :] = jnp.zeros((ROWS, 128), BF16)
                g_all[pair, rows, :] = jnp.zeros((ROWS, 128), BF16)
            mask_in[flow] = jnp.full((8, 128), MASKED, F32)
            part_in[flow] = jnp.full((CHUNKS, 8, TILE), MASKED, F32)
            final_in[flow] = jnp.zeros((CHUNKS, 8, TILE), F32)
            dq_in[flow] = jnp.zeros((CHUNKS, 128, TILE), BF16)

    inner = receives[0] & receives[1]

    @pl.when(inner)
    def _():
        pl.semaphore_wait(barrier, 2)

    @pl.when(jnp.logical_not(inner))
    def _():
        pl.semaphore_wait(barrier, 1)

    def remote(source, place, send_sem, recv_sem, flow):
        return pltpu.make_async_remote_copy(
            src_ref=source,
            dst_ref=place,
            send_sem=send_sem,
            recv_sem=recv_sem,
            device_id={"patch": target[flow]},
            device_id_type=MESH,
        )

    def mask_copy(flow):
        return remote(
            mask_out.at[flow], mask_in.at[flow], mask_send.at[flow], mask_recv.at[flow], flow
        )

    def split(chunk):
        pair = lax.div(chunk, 2)
        first = pl.multiple_of(lax.rem(chunk, 2) * TILE, TILE)
        return pair, first

    def bulk_copy(chunk, flow, array):
        pair, first = split(chunk)
        lanes = pl.ds(pl.multiple_of(pair * 128, 128), 128)
        source = (query, gout)[array].at[pl.ds(first, TILE), lanes]
        place = (q_all, g_all)[array].at[pair, pl.ds(2 * ROWS * flow + first, TILE)]
        at = (flow, chunk, array)
        return remote(source, place, bulk_send.at[at], bulk_recv.at[at], flow)

    def part_copy(chunk, flow):
        at = (flow, chunk)
        return remote(part_out.at[at], part_in.at[at], part_send.at[at], part_recv.at[at], flow)

    def final_copy(chunk, flow):
        at = (flow, chunk)
        return remote(
            final_out.at[chunk], final_in.at[at], final_send.at[at], final_recv.at[at], flow
        )

    def dq_copy(chunk, flow):
        at = (flow, chunk)
        return remote(dq_out.at[at], dq_in.at[at], dq_send.at[at], dq_recv.at[at], flow)

    def start(copies):
        for flow in (0, 1):

            @pl.when(sends[flow])
            def _(flow=flow):
                for copy in copies(flow):
                    copy.start()

    def wait_send(copies):
        for flow in (0, 1):

            @pl.when(sends[flow])
            def _(flow=flow):
                for copy in copies(flow):
                    copy.wait_send()

    def wait_recv(copies):
        for flow in (0, 1):

            @pl.when(receives[flow])
            def _(flow=flow):
                for copy in copies(flow):
                    copy.wait_recv()

    def bulk_copies(chunk):
        return lambda flow: [bulk_copy(chunk, flow, array) for array in (0, 1)]

    start(lambda flow: [mask_copy(flow)])
    for chunk in range(AHEAD):
        start(bulk_copies(jnp.int32(chunk)))

    for pair in range(PAIRS):
        for array in range(4):
            load(pair, array).wait()
    for pair in range(PAIRS):
        k_turned[pair] = k_pair[pair].T

    half = lax.broadcasted_iota(jnp.int32, (1, 128), 1) < 64
    halves = (half, jnp.logical_not(half))

    def keys_of(pair, h):
        return (
            jnp.where(halves[h], k_pair[pair], hot[...]),
            jnp.where(halves[h], v_pair[pair], jnp.zeros((), BF16)),
        )

    def scores_of(keys, values, pair, rows, h, e_ref, d_ref):
        queries = jnp.where(halves[h], q_all[pair, rows, :], bias[rows, :])
        scores = dot_last(keys, queries)
        peak = jnp.max(scores, axis=0, keepdims=True)
        raised = jnp.exp2((scores - peak) * base2)
        e_ref[...] = raised
        dweights = dot_last(values, g_all[pair, rows, :])
        d_ref[...] = dweights
        total = jnp.sum(raised, axis=0, keepdims=True)
        weighted = jnp.sum(raised * dweights, axis=0, keepdims=True)
        return [peak, total, weighted]

    def rows_of(found):
        return jnp.concatenate(found + [jnp.zeros((1, TILE), F32)] * (8 - len(found)), axis=0)

    def own_scores(pair, carry):
        both = [keys_of(pair, h) for h in (0, 1)]
        for t in (0, 1):
            chunk = 2 * pair + t
            found = []
            for h in (0, 1):
                rows = pl.ds(ROWS + TILE * t, TILE)
                found += scores_of(
                    *both[h], pair, rows, h, e_own.at[chunk, h], d_own.at[chunk, h]
                )
            part_own[chunk] = rows_of(found)
        return carry

    lax.fori_loop(0, PAIRS, own_scores, 0)

    wait_recv(lambda flow: [mask_copy(flow)])
    spread(0, mask_in[0])
    spread(2, mask_in[1])

    def near_scores(chunk):
        pair, first = split(chunk)
        slot = lax.rem(chunk, RING)
        found = [[], []]
        for h in (0, 1):
            keys, values = keys_of(pair, h)
            for side in (0, 1):
                rows = pl.ds(2 * ROWS * side + first, TILE)
                found[side] += scores_of(
                    keys, values, pair, rows, h, e_near.at[slot, side, h], d_near.at[slot, side, h]
                )
        part_out[1, chunk] = rows_of(found[0])
        part_out[0, chunk] = rows_of(found[1])

    def combine(chunk):
        parts = [part_own[chunk], part_in[0, chunk], part_in[1, chunk]]
        found = []
        for h in (0, 1):
            peaks, totals, sums = (
                [part[3 * h + i : 3 * h + i + 1, :] for part in parts] for i in range(3)
            )
            top = functools.reduce(jnp.maximum, peaks)
            scales = [jnp.exp2((peak - top) * base2) for peak in peaks]
            total = sum(scale * one for scale, one in zip(scales, totals))
            delta = sum(scale * one for scale, one in zip(scales, sums)) / total
            found += [top * base2 + jnp.log2(total), delta]
        final_out[chunk] = rows_of(found)

    def finish(chunk):
        pair, first = split(chunk)
        slot = lax.rem(chunk, RING)
        for h in (0, 1):
            turned = k_turned[pair, pl.ds(64 * h, 64), :]
            for block in range(3):
                side = block // 2
                if block == 1:
                    e_ref, d_ref = e_own.at[chunk, h], d_own.at[chunk, h]
                    peaks, finals = part_own.at[chunk], final_out.at[chunk]
                else:
                    e_ref, d_ref = e_near.at[slot, side, h], d_near.at[slot, side, h]
                    peaks, finals = part_out.at[1 - side, chunk], final_in.at[side, chunk]
                peak = peaks[3 * h : 3 * h + 1, :]
                log_total = finals[2 * h : 2 * h + 1, :]
                delta = finals[2 * h + 1 : 2 * h + 2, :]
                weight = e_ref[...] * jnp.exp2(peak * base2 - log_total)
                dscore = (weight * (d_ref[...] - delta)).astype(BF16)
                lanes = pl.ds(ROWS * block + first, TILE)
                weights[h, :, lanes] = weight.astype(BF16)
                dscores[h, :, lanes] = dscore
                part = dot(turned, dscore)
                if block == 1:
                    dq_own[chunk, pl.ds(64 * h, 64), :] = part
                else:
                    dq_out[1 - side, chunk, pl.ds(64 * h, 64), :] = part.astype(BF16)

    def store(which, pair):
        lanes = pl.ds(pl.multiple_of(pair * 128, 128), 128)
        source = (dk_done, dv_done)[which].at[pair]
        place = (grad_key, grad_value)[which].at[:, lanes]
        return pltpu.make_async_copy(source, place, store_sem.at[which, pair])

    def store_query(chunk):
        pair, first = split(chunk)
        lanes = pl.ds(pl.multiple_of(pair * 128, 128), 128)
        place = grad_query.at[pl.ds(first, TILE), lanes]
        return pltpu.make_async_copy(dq_done.at[chunk], place, store_sem.at[2, chunk])

    def key_gradients(pair):
        dv = [dot(weights[h], g_all[pair]) for h in (0, 1)]
        dk = [dot(dscores[h], q_all[pair]) for h in (0, 1)]
        dv_done[pair] = jnp.where(half, dv[0], dv[1]).astype(BF16)
        dk_done[pair] = (jnp.where(half, dk[0], dk[1]) * scaling).astype(BF16)

    def query_gradients(chunk):
        total = dq_own[chunk] + dq_in[0, chunk].astype(F32) + dq_in[1, chunk].astype(F32)
        dq_done[chunk] = (total * scaling).T.astype(BF16)

    def step(s, carry):
        @pl.when(s < CHUNKS)
        def _():
            wait_recv(bulk_copies(s))

            @pl.when(s + AHEAD < CHUNKS)
            def _():
                start(bulk_copies(s + AHEAD))

            near_scores(s)
            start(lambda flow: [part_copy(s, flow)])

        @pl.when((s >= LAG_B) & (s < CHUNKS + LAG_B))
        def _():
            chunk = s - LAG_B
            wait_recv(lambda flow: [part_copy(chunk, flow)])
            combine(chunk)
            start(lambda flow: [final_copy(chunk, flow)])

        @pl.when((s >= LAG_C) & (s < CHUNKS + LAG_C))
        def _():
            chunk = s - LAG_C
            wait_recv(lambda flow: [final_copy(chunk, flow)])
            finish(chunk)
            start(lambda flow: [dq_copy(chunk, flow)])

            @pl.when(lax.rem(chunk, 2) == 1)
            def _():
                pair = lax.div(chunk, 2)
                key_gradients(pair)
                store(0, pair).start()
                store(1, pair).start()

        @pl.when(s >= LAG_D)
        def _():
            chunk = s - LAG_D
            wait_recv(lambda flow: [dq_copy(chunk, flow)])
            query_gradients(chunk)
            store_query(chunk).start()

        return carry

    lax.fori_loop(0, CHUNKS + LAG_D, step, 0)

    wait_send(lambda flow: [mask_copy(flow)])

    def drain(chunk, carry):
        wait_send(
            lambda flow: [
                *bulk_copies(chunk)(flow),
                part_copy(chunk, flow),
                final_copy(chunk, flow),
                dq_copy(chunk, flow),
            ]
        )
        store_query(chunk).wait()
        return carry

    lax.fori_loop(0, CHUNKS, drain, 0)
    for pair in range(PAIRS):
        store(0, jnp.int32(pair)).wait()
        store(1, jnp.int32(pair)).wait()


def body(n, query_rows, key_rows, value_rows, grad_output, neighbours, owner):
    rows, features = query_rows.shape
    out = jax.ShapeDtypeStruct((rows, features), BF16)
    whole = pl.BlockSpec(memory_space=pl.ANY)
    dma = pltpu.SemaphoreType.DMA
    wide = ROWS * 3
    return pl.pallas_call(
        functools.partial(kernel, n),
        out_shape=[out] * 3,
        in_specs=[whole] * 6,
        out_specs=[whole] * 3,
        scratch_shapes=[
            pltpu.SMEM(owner.shape, jnp.int32),
            pltpu.VMEM(neighbours.shape, jnp.int32),
            pltpu.VMEM((PAIRS, ROWS, 128), BF16),
            pltpu.VMEM((PAIRS, ROWS, 128), BF16),
            pltpu.VMEM((PAIRS, 128, ROWS), BF16),
            pltpu.VMEM((PAIRS, wide, 128), BF16),
            pltpu.VMEM((PAIRS, wide, 128), BF16),
            pltpu.VMEM((wide, 128), BF16),
            pltpu.VMEM((ROWS, 128), BF16),
            pltpu.VMEM((2, 8, 128), F32),
            pltpu.VMEM((2, 8, 128), F32),
            pltpu.VMEM((CHUNKS, 2, ROWS, TILE), F32),
            pltpu.VMEM((CHUNKS, 2, ROWS, TILE), F32),
            pltpu.VMEM((RING, 2, 2, ROWS, TILE), F32),
            pltpu.VMEM((RING, 2, 2, ROWS, TILE), F32),
            pltpu.VMEM((CHUNKS, 8, TILE), F32),
            pltpu.VMEM((2, CHUNKS, 8, TILE), F32),
            pltpu.VMEM((2, CHUNKS, 8, TILE), F32),
            pltpu.VMEM((CHUNKS, 8, TILE), F32),
            pltpu.VMEM((2, CHUNKS, 8, TILE), F32),
            pltpu.VMEM((2, ROWS, wide), BF16),
            pltpu.VMEM((2, ROWS, wide), BF16),
            pltpu.VMEM((CHUNKS, 128, TILE), F32),
            pltpu.VMEM((2, CHUNKS, 128, TILE), BF16),
            pltpu.VMEM((2, CHUNKS, 128, TILE), BF16),
            pltpu.VMEM((CHUNKS, TILE, 128), BF16),
            pltpu.VMEM((PAIRS, ROWS, 128), BF16),
            pltpu.VMEM((PAIRS, ROWS, 128), BF16),
            dma((4 * PAIRS + 2,)),
            dma((2, CHUNKS, 2)),
            dma((2, CHUNKS, 2)),
            dma((2,)),
            dma((2,)),
            dma((2, CHUNKS)),
            dma((2, CHUNKS)),
            dma((2, CHUNKS)),
            dma((2, CHUNKS)),
            dma((2, CHUNKS)),
            dma((2, CHUNKS)),
            dma((3, CHUNKS)),
        ],
        compiler_params=pltpu.CompilerParams(
            collective_id=0, has_side_effects=True, vmem_limit_bytes=60 << 20
        ),
    )(query_rows, key_rows, value_rows, grad_output, neighbours, owner)


def solution(mesh):
    split = P(("scene", "patch"), None)
    return jax.shard_map(
        functools.partial(body, mesh.shape["patch"]),
        mesh=mesh,
        in_specs=(split, split, split, split, split, P("scene")),
        out_specs=(split, split, split),
        check_vma=False,
    )
```

```python
import functools
import math

import jax
import jax.numpy as jnp
from jax import lax
from jax.experimental import pallas as pl
from jax.experimental.pallas import tpu as pltpu
from jax.sharding import PartitionSpec as P

HEADS = 8
MESH = pl.DeviceIdType.MESH
BF16, F32 = jnp.bfloat16, jnp.float32
MASKED = -1e30
ROWS = 512
TILE = 256
PAIRS = 4
CHUNKS = PAIRS * ROWS // TILE
RING = 4
LAG_C, LAG_D = 3, 6
AHEAD = 3


def dot(left, right):
    return lax.dot_general(left, right, (((1,), (0,)), ((), ())), preferred_element_type=F32)


def dot_last(left, right):
    return lax.dot_general(left, right, (((1,), (1,)), ((), ())), preferred_element_type=F32)


def kernel(
    n,
    query, key, value, gout, neighbours, owner,
    grad_query, grad_key, grad_value,
    own_ids, near_ids, k_pair, v_pair, k_turned, q_all, g_all, bias, hot, mask_out, mask_in,
    e_own, d_own, e_near, d_near, peaks, stat_out, stat_in, stat_far,
    weights, dscores, dq_own, dq_out, dq_in,
    load_sem, bulk_send, bulk_recv, mask_send, mask_recv, stat_send, stat_recv,
    far_send, far_recv, dq_send, dq_recv,
):
    me = lax.axis_index("patch")
    target = (jnp.minimum(me + 1, n - 1), jnp.maximum(me - 1, 0))
    sends = (me < n - 1, me > 0)
    receives = (me > 0, me < n - 1)
    far_target = (jnp.minimum(me + 2, n - 1), jnp.maximum(me - 2, 0))
    far_sends = (me < n - 2, me > 1)
    far_receives = (me > 1, me < n - 2)
    scaling = 1.0 / math.sqrt(64)
    base2 = scaling * math.log2(math.e)

    barrier = pltpu.get_barrier_semaphore()
    peers = jnp.int32(0)
    for exists, peer in zip(sends + far_sends, target + far_target):
        peers = peers + exists.astype(jnp.int32)

        @pl.when(exists)
        def _(peer=peer):
            pl.semaphore_signal(barrier, inc=1, device_id={"patch": peer}, device_id_type=MESH)

    own_copy = pltpu.make_async_copy(owner, own_ids, load_sem.at[4 * PAIRS])
    near_copy = pltpu.make_async_copy(neighbours, near_ids, load_sem.at[4 * PAIRS + 1])
    own_copy.start()
    near_copy.start()

    def load(pair, array):
        lanes = pl.ds(128 * pair, 128)
        middle = pl.ds(ROWS, ROWS)
        source = (key, value, query, gout)[array].at[:, lanes]
        place = (
            k_pair.at[pair],
            v_pair.at[pair],
            q_all.at[pair, middle],
            g_all.at[pair, middle],
        )[array]
        return pltpu.make_async_copy(source, place, load_sem.at[4 * pair + array])

    for pair in range(PAIRS):
        for array in range(4):
            load(pair, array).start()

    pl.semaphore_wait(barrier, peers)

    def remote(source, place, send_sem, recv_sem, flow):
        return pltpu.make_async_remote_copy(
            src_ref=source,
            dst_ref=place,
            send_sem=send_sem,
            recv_sem=recv_sem,
            device_id={"patch": target[flow]},
            device_id_type=MESH,
        )

    def mask_copy(flow):
        return remote(
            mask_out.at[flow], mask_in.at[flow], mask_send.at[flow], mask_recv.at[flow], flow
        )

    def split(chunk):
        pair = lax.div(chunk, 2)
        first = pl.multiple_of(lax.rem(chunk, 2) * TILE, TILE)
        return pair, first

    def bulk_copy(chunk, flow, array):
        pair, first = split(chunk)
        lanes = pl.ds(pl.multiple_of(pair * 128, 128), 128)
        source = (query, gout)[array].at[pl.ds(first, TILE), lanes]
        place = (q_all, g_all)[array].at[pair, pl.ds(2 * ROWS * flow + first, TILE)]
        at = (flow, chunk, array)
        return remote(source, place, bulk_send.at[at], bulk_recv.at[at], flow)

    def stat_copy(chunk, flow):
        at = (flow, chunk)
        return remote(stat_out.at[at], stat_in.at[at], stat_send.at[at], stat_recv.at[at], flow)

    def far_copy(chunk, flow):
        at = (flow, chunk)
        return pltpu.make_async_remote_copy(
            src_ref=stat_out.at[flow, chunk, 1],
            dst_ref=stat_far.at[at],
            send_sem=far_send.at[at],
            recv_sem=far_recv.at[at],
            device_id={"patch": far_target[flow]},
            device_id_type=MESH,
        )

    def dq_copy(chunk, flow):
        at = (flow, chunk)
        return remote(dq_out.at[at], dq_in.at[at], dq_send.at[at], dq_recv.at[at], flow)

    def start(copies, when=sends):
        for flow in (0, 1):

            @pl.when(when[flow])
            def _(flow=flow):
                for copy in copies(flow):
                    copy.start()

    def wait_send(copies, when=sends):
        for flow in (0, 1):

            @pl.when(when[flow])
            def _(flow=flow):
                for copy in copies(flow):
                    copy.wait_send()

    def wait_recv(copies, when=receives):
        for flow in (0, 1):

            @pl.when(when[flow])
            def _(flow=flow):
                for copy in copies(flow):
                    copy.wait_recv()

    def bulk_copies(chunk):
        return lambda flow: [bulk_copy(chunk, flow, array) for array in (0, 1)]

    start(bulk_copies(jnp.int32(0)))

    own_copy.wait()
    near_copy.wait()
    lane = lax.broadcasted_iota(jnp.int32, (8, 128), 1)
    low_lane = lax.rem(lane, 64)
    first_id = 8 * (me - 1)
    held = [jnp.full((8, 128), -1, jnp.int32) for _ in range(3)]
    for t in range(24):
        number = first_id + t
        valid = (number >= 0) & (number < 8 * n)
        slot = own_ids[jnp.clip(number, 0, 8 * n - 1)] - first_id
        slot = jnp.where(valid, slot, -1000)
        held = [jnp.where(low_lane == slot - 8 * w, number, held[w]) for w in range(3)]
    near = near_ids[...]
    found = [jnp.zeros((8, 128), jnp.bool_) for _ in range(3)]
    for j in range(16):
        column = jnp.broadcast_to(near[:, j : j + 1], (8, 128))
        found = [found[w] | (column == held[w]) for w in range(3)]
    masks = [jnp.where(found[w] | (low_lane >= 8), 0.0, MASKED) for w in range(3)]
    mask_out[0] = masks[2]
    mask_out[1] = masks[0]
    start(lambda flow: [mask_copy(flow)])
    for chunk in range(1, AHEAD):
        start(bulk_copies(jnp.int32(chunk)))

    def spread(block, mask):
        for a in range(8):
            rows = pl.ds(ROWS * block + 64 * a, 64)
            bias[rows, :] = jnp.broadcast_to(mask[a : a + 1, :], (64, 128)).astype(BF16)

    spread(1, masks[1])
    row_slot = lax.broadcasted_iota(jnp.int32, (ROWS, 128), 0) // 64
    lane_slot = lax.rem(lax.broadcasted_iota(jnp.int32, (ROWS, 128), 1), 64)
    hot[...] = jnp.where(row_slot == lane_slot, 1.0, 0.0).astype(BF16)

    for flow in (0, 1):

        @pl.when(jnp.logical_not(receives[flow]))
        def _(flow=flow):
            rows = pl.ds(2 * ROWS * flow, ROWS)
            for pair in range(PAIRS):
                q_all[pair, rows, :] = jnp.zeros((ROWS, 128), BF16)
                g_all[pair, rows, :] = jnp.zeros((ROWS, 128), BF16)
            mask_in[flow] = jnp.full((8, 128), MASKED, F32)
            stat_in[flow] = jnp.full((CHUNKS, 2, 8, 128), MASKED, F32)
            dq_in[flow] = jnp.zeros((CHUNKS, 128, TILE), BF16)

        @pl.when(jnp.logical_not(far_receives[flow]))
        def _(flow=flow):
            stat_far[flow] = jnp.full((CHUNKS, 8, 128), MASKED, F32)

    for pair in range(PAIRS):
        for array in range(4):
            load(pair, array).wait()
    for pair in range(PAIRS):
        k_turned[pair] = k_pair[pair].T

    half = lax.broadcasted_iota(jnp.int32, (1, 128), 1) < 64
    halves = (half, jnp.logical_not(half))

    def keys_of(pair, h):
        return (
            jnp.where(halves[h], k_pair[pair], hot[...]),
            jnp.where(halves[h], v_pair[pair], jnp.zeros((), BF16)),
        )

    def scores_of(keys, values, pair, rows, h, e_ref, d_ref):
        queries = jnp.where(halves[h], q_all[pair, rows, :], bias[rows, :])
        scores = dot_last(keys, queries)
        peak = jnp.max(scores, axis=0, keepdims=True)
        raised = jnp.exp2((scores - peak) * base2)
        e_ref[...] = raised
        dweights = dot_last(values, g_all[pair, rows, :])
        d_ref[...] = dweights
        total = jnp.sum(raised, axis=0, keepdims=True)
        weighted = jnp.sum(raised * dweights, axis=0, keepdims=True)
        raised_by = peak * base2
        return raised_by, raised_by + jnp.log2(total), weighted / total

    def packed(found):
        rows = [row for peak, log_total, delta in found for row in halved(log_total)]
        rows += [row for peak, log_total, delta in found for row in halved(delta)]
        return jnp.concatenate(rows, axis=0)

    def halved(row):
        return [row[:, :128], row[:, 128:]]

    def keep_peaks(block, chunk, found):
        for h in (0, 1):
            peaks[block, chunk, h : h + 1, :] = found[h][0]

    def own_scores(pair, carry):
        both = [keys_of(pair, h) for h in (0, 1)]
        for t in (0, 1):
            chunk = 2 * pair + t
            found = []
            for h in (0, 1):
                rows = pl.ds(ROWS + TILE * t, TILE)
                found += [
                    scores_of(*both[h], pair, rows, h, e_own.at[chunk, h], d_own.at[chunk, h])
                ]
            keep_peaks(1, chunk, found)
            stat_out[0, chunk, 0] = packed(found)
            stat_out[1, chunk, 0] = packed(found)
        return carry

    lax.fori_loop(0, PAIRS, own_scores, 0)

    wait_recv(lambda flow: [mask_copy(flow)])
    spread(0, mask_in[0])
    spread(2, mask_in[1])

    def near_scores(chunk):
        pair, first = split(chunk)
        slot = lax.rem(chunk, RING)
        found = [[], []]
        for h in (0, 1):
            keys, values = keys_of(pair, h)
            for side in (0, 1):
                rows = pl.ds(2 * ROWS * side + first, TILE)
                e_ref, d_ref = e_near.at[slot, side, h], d_near.at[slot, side, h]
                found[side] += [scores_of(keys, values, pair, rows, h, e_ref, d_ref)]
        for side in (0, 1):
            keep_peaks(2 * side, chunk, found[side])
            stat_out[1 - side, chunk, 1] = packed(found[side])

    def combined(parts):
        logs, deltas = [part[:4] for part in parts], [part[4:] for part in parts]
        top = functools.reduce(jnp.maximum, logs)
        scales = [jnp.exp2(one - top) for one in logs]
        total = sum(scales)
        delta = sum(scale * one for scale, one in zip(scales, deltas)) / total
        return top + jnp.log2(total), delta

    def finish(chunk):
        pair, first = split(chunk)
        slot = lax.rem(chunk, RING)
        finals = [
            combined([stat_out[1, chunk, 1], stat_in[0, chunk, 0], stat_far[0, chunk]]),
            combined([stat_out[0, chunk, 0], stat_in[0, chunk, 1], stat_in[1, chunk, 1]]),
            combined([stat_out[0, chunk, 1], stat_in[1, chunk, 0], stat_far[1, chunk]]),
        ]
        for h in (0, 1):
            turned = k_turned[pair, pl.ds(64 * h, 64), :]
            for block in range(3):
                side = block // 2
                if block == 1:
                    e_ref, d_ref = e_own.at[chunk, h], d_own.at[chunk, h]
                else:
                    e_ref, d_ref = e_near.at[slot, side, h], d_near.at[slot, side, h]
                log_total, delta = (
                    jnp.concatenate([one[2 * h : 2 * h + 1], one[2 * h + 1 : 2 * h + 2]], axis=1)
                    for one in finals[block]
                )
                weight = e_ref[...] * jnp.exp2(peaks[block, chunk, h : h + 1, :] - log_total)
                dscore = (weight * (d_ref[...] - delta)).astype(BF16)
                lanes = pl.ds(ROWS * block + first, TILE)
                weights[h, :, lanes] = weight.astype(BF16)
                dscores[h, :, lanes] = dscore
                part = dot(turned, dscore)
                if block == 1:
                    dq_own[chunk, pl.ds(64 * h, 64), :] = part
                else:
                    dq_out[1 - side, chunk, pl.ds(64 * h, 64), :] = part.astype(BF16)

    def key_gradients(pair):
        dv = [dot(weights[h], g_all[pair]) for h in (0, 1)]
        dk = [dot(dscores[h], q_all[pair]) for h in (0, 1)]
        grad_value[pair] = jnp.where(half, dv[0], dv[1]).astype(BF16)
        grad_key[pair] = (jnp.where(half, dk[0], dk[1]) * scaling).astype(BF16)

    def query_gradients(chunk):
        total = dq_own[chunk] + dq_in[0, chunk].astype(F32) + dq_in[1, chunk].astype(F32)
        grad_query[chunk] = (total * scaling).T.astype(BF16)

    def step(s, carry):
        @pl.when(s < CHUNKS)
        def _():
            wait_recv(bulk_copies(s))
            near_scores(s)
            start(lambda flow: [stat_copy(s, flow)])
            start(lambda flow: [far_copy(s, flow)], far_sends)

            @pl.when(s + AHEAD < CHUNKS)
            def _():
                start(bulk_copies(s + AHEAD))

        @pl.when((s >= LAG_C) & (s < CHUNKS + LAG_C))
        def _():
            chunk = s - LAG_C
            wait_recv(lambda flow: [stat_copy(chunk, flow)])
            wait_recv(lambda flow: [far_copy(chunk, flow)], far_receives)
            finish(chunk)

            @pl.when(chunk == 1)
            def _():
                start(lambda flow: [dq_copy(0, flow)])

            @pl.when(chunk >= 1)
            def _():
                start(lambda flow: [dq_copy(chunk, flow)])

            @pl.when(lax.rem(chunk, 2) == 1)
            def _():
                key_gradients(lax.div(chunk, 2))

        @pl.when(s >= LAG_D)
        def _():
            chunk = s - LAG_D
            wait_recv(lambda flow: [dq_copy(chunk, flow)])
            query_gradients(chunk)

        return carry

    lax.fori_loop(0, CHUNKS + LAG_D, step, 0)

    wait_send(lambda flow: [mask_copy(flow)])

    def drain(chunk, carry):
        wait_send(
            lambda flow: [
                *bulk_copies(chunk)(flow),
                stat_copy(chunk, flow),
                dq_copy(chunk, flow),
            ]
        )
        wait_send(lambda flow: [far_copy(chunk, flow)], far_sends)
        return carry

    lax.fori_loop(0, CHUNKS, drain, 0)


def write_out(dq, dk, dv, grad_query, grad_key, grad_value, sem):
    copies = []
    for chunk in range(CHUNKS):
        place = (pl.ds(TILE * (chunk % 2), TILE), pl.ds(128 * (chunk // 2), 128))
        copies.append((dq.at[chunk], grad_query.at[place]))
    for pair in range(PAIRS):
        place = (slice(None), pl.ds(128 * pair, 128))
        copies.append((dk.at[pair], grad_key.at[place]))
        copies.append((dv.at[pair], grad_value.at[place]))
    copies = [pltpu.make_async_copy(*one, sem.at[i]) for i, one in enumerate(copies)]
    for copy in copies:
        copy.start()
    for copy in copies:
        copy.wait()


def body(n, query_rows, key_rows, value_rows, grad_output, neighbours, owner):
    rows, features = query_rows.shape
    out = jax.ShapeDtypeStruct((rows, features), BF16)
    far, near = pl.BlockSpec(memory_space=pl.ANY), pl.BlockSpec(memory_space=pltpu.VMEM)
    dma = pltpu.SemaphoreType.DMA
    wide = ROWS * 3
    parts = pl.pallas_call(
        functools.partial(kernel, n),
        out_shape=[
            jax.ShapeDtypeStruct((CHUNKS, TILE, 128), BF16),
            jax.ShapeDtypeStruct((PAIRS, ROWS, 128), BF16),
            jax.ShapeDtypeStruct((PAIRS, ROWS, 128), BF16),
        ],
        in_specs=[far] * 6,
        out_specs=[near] * 3,
        scratch_shapes=[
            pltpu.SMEM(owner.shape, jnp.int32),
            pltpu.VMEM(neighbours.shape, jnp.int32),
            pltpu.VMEM((PAIRS, ROWS, 128), BF16),
            pltpu.VMEM((PAIRS, ROWS, 128), BF16),
            pltpu.VMEM((PAIRS, 128, ROWS), BF16),
            pltpu.VMEM((PAIRS, wide, 128), BF16),
            pltpu.VMEM((PAIRS, wide, 128), BF16),
            pltpu.VMEM((wide, 128), BF16),
            pltpu.VMEM((ROWS, 128), BF16),
            pltpu.VMEM((2, 8, 128), F32),
            pltpu.VMEM((2, 8, 128), F32),
            pltpu.VMEM((CHUNKS, 2, ROWS, TILE), F32),
            pltpu.VMEM((CHUNKS, 2, ROWS, TILE), F32),
            pltpu.VMEM((RING, 2, 2, ROWS, TILE), F32),
            pltpu.VMEM((RING, 2, 2, ROWS, TILE), F32),
            pltpu.VMEM((3, CHUNKS, 8, TILE), F32),
            pltpu.VMEM((2, CHUNKS, 2, 8, 128), F32),
            pltpu.VMEM((2, CHUNKS, 2, 8, 128), F32),
            pltpu.VMEM((2, CHUNKS, 8, 128), F32),
            pltpu.VMEM((2, ROWS, wide), BF16),
            pltpu.VMEM((2, ROWS, wide), BF16),
            pltpu.VMEM((CHUNKS, 128, TILE), F32),
            pltpu.VMEM((2, CHUNKS, 128, TILE), BF16),
            pltpu.VMEM((2, CHUNKS, 128, TILE), BF16),
            dma((4 * PAIRS + 2,)),
            dma((2, CHUNKS, 2)),
            dma((2, CHUNKS, 2)),
            dma((2,)),
            dma((2,)),
            dma((2, CHUNKS)),
            dma((2, CHUNKS)),
            dma((2, CHUNKS)),
            dma((2, CHUNKS)),
            dma((2, CHUNKS)),
            dma((2, CHUNKS)),
        ],
        compiler_params=pltpu.CompilerParams(
            collective_id=0, has_side_effects=True, vmem_limit_bytes=56 << 20
        ),
    )(query_rows, key_rows, value_rows, grad_output, neighbours, owner)
    return pl.pallas_call(
        write_out,
        out_shape=[out] * 3,
        in_specs=[near] * 3,
        out_specs=[far] * 3,
        scratch_shapes=[dma((CHUNKS + 2 * PAIRS,))],
    )(*parts)


def solution(mesh):
    split = P(("scene", "patch"), None)
    return jax.shard_map(
        functools.partial(body, mesh.shape["patch"]),
        mesh=mesh,
        in_specs=(split, split, split, split, split, P("scene")),
        out_specs=(split, split, split),
        check_vma=False,
    )
```

```python
import functools
import math

import jax
import jax.numpy as jnp
from jax import lax
from jax.experimental import pallas as pl
from jax.experimental.pallas import tpu as pltpu
from jax.sharding import PartitionSpec as P

HEADS = 8
MESH = pl.DeviceIdType.MESH
BF16, F32 = jnp.bfloat16, jnp.float32
MASKED = -1e30
ROWS = 512
TILE = 256
PAIRS = 4
CHUNKS = PAIRS * ROWS // TILE
RING = 4
LAG_C, LAG_D = 3, 7
AHEAD = 3


def dot(left, right):
    return lax.dot_general(left, right, (((1,), (0,)), ((), ())), preferred_element_type=F32)


def dot_last(left, right):
    return lax.dot_general(left, right, (((1,), (1,)), ((), ())), preferred_element_type=F32)


def kernel(
    n,
    query, key, value, gout, neighbours, owner,
    grad_query, grad_key, grad_value,
    own_ids, near_ids, k_pair, v_pair, k_turned, q_all, g_all, bias, hot, mask_out, mask_in,
    e_own, d_own, e_near, d_near, peaks, stat_out, stat_in, stat_far,
    weights, dscores, dq_own, dq_out, dq_in,
    load_sem, bulk_send, bulk_recv, mask_send, mask_recv, stat_send, stat_recv,
    far_send, far_recv, dq_send, dq_recv,
):
    me = lax.axis_index("patch")
    target = (jnp.minimum(me + 1, n - 1), jnp.maximum(me - 1, 0))
    sends = (me < n - 1, me > 0)
    receives = (me > 0, me < n - 1)
    far_target = (jnp.minimum(me + 2, n - 1), jnp.maximum(me - 2, 0))
    far_sends = (me < n - 2, me > 1)
    far_receives = (me > 1, me < n - 2)
    scaling = 1.0 / math.sqrt(64)
    base2 = scaling * math.log2(math.e)

    barrier = pltpu.get_barrier_semaphore()
    peers = jnp.int32(0)
    for exists, peer in zip(sends + far_sends, target + far_target):
        peers = peers + exists.astype(jnp.int32)

        @pl.when(exists)
        def _(peer=peer):
            pl.semaphore_signal(barrier, inc=1, device_id={"patch": peer}, device_id_type=MESH)

    own_copy = pltpu.make_async_copy(owner, own_ids, load_sem.at[4 * PAIRS])
    near_copy = pltpu.make_async_copy(neighbours, near_ids, load_sem.at[4 * PAIRS + 1])
    own_copy.start()
    near_copy.start()

    def load(pair, array):
        lanes = pl.ds(128 * pair, 128)
        middle = pl.ds(ROWS, ROWS)
        source = (key, value, query, gout)[array].at[:, lanes]
        place = (
            k_pair.at[pair],
            v_pair.at[pair],
            q_all.at[pair, middle],
            g_all.at[pair, middle],
        )[array]
        return pltpu.make_async_copy(source, place, load_sem.at[4 * pair + array])

    pl.semaphore_wait(barrier, peers)

    def remote(source, place, send_sem, recv_sem, flow):
        return pltpu.make_async_remote_copy(
            src_ref=source,
            dst_ref=place,
            send_sem=send_sem,
            recv_sem=recv_sem,
            device_id={"patch": target[flow]},
            device_id_type=MESH,
        )

    def mask_copy(flow):
        return remote(
            mask_out.at[flow], mask_in.at[flow], mask_send.at[flow], mask_recv.at[flow], flow
        )

    def split(chunk):
        pair = lax.div(chunk, 2)
        first = pl.multiple_of(lax.rem(chunk, 2) * TILE, TILE)
        return pair, first

    def bulk_copy(chunk, flow, array):
        pair, first = split(chunk)
        lanes = pl.ds(pl.multiple_of(pair * 128, 128), 128)
        source = (query, gout)[array].at[pl.ds(first, TILE), lanes]
        place = (q_all, g_all)[array].at[pair, pl.ds(2 * ROWS * flow + first, TILE)]
        at = (flow, chunk, array)
        return remote(source, place, bulk_send.at[at], bulk_recv.at[at], flow)

    def stat_copy(chunk, flow):
        at = (flow, chunk)
        return remote(stat_out.at[at], stat_in.at[at], stat_send.at[at], stat_recv.at[at], flow)

    def far_copy(chunk, flow):
        at = (flow, chunk)
        return pltpu.make_async_remote_copy(
            src_ref=stat_out.at[flow, chunk, 1],
            dst_ref=stat_far.at[at],
            send_sem=far_send.at[at],
            recv_sem=far_recv.at[at],
            device_id={"patch": far_target[flow]},
            device_id_type=MESH,
        )

    def dq_copy(chunk, flow, h):
        at = (flow, chunk, h)
        return remote(dq_out.at[at], dq_in.at[at], dq_send.at[at], dq_recv.at[at], flow)

    def start(copies, when=sends):
        for flow in (0, 1):

            @pl.when(when[flow])
            def _(flow=flow):
                for copy in copies(flow):
                    copy.start()

    def wait_send(copies, when=sends):
        for flow in (0, 1):

            @pl.when(when[flow])
            def _(flow=flow):
                for copy in copies(flow):
                    copy.wait_send()

    def wait_recv(copies, when=receives):
        for flow in (0, 1):

            @pl.when(when[flow])
            def _(flow=flow):
                for copy in copies(flow):
                    copy.wait_recv()

    def bulk_copies(chunk):
        return lambda flow: [bulk_copy(chunk, flow, array) for array in (0, 1)]

    start(bulk_copies(jnp.int32(0)))

    for pair in range(PAIRS):
        for array in range(4):
            load(pair, array).start()

    own_copy.wait()
    near_copy.wait()
    lane = lax.broadcasted_iota(jnp.int32, (8, 128), 1)
    low_lane = lax.rem(lane, 64)
    first_id = 8 * (me - 1)
    held = [jnp.full((8, 128), -1, jnp.int32) for _ in range(3)]
    for t in range(24):
        number = first_id + t
        valid = (number >= 0) & (number < 8 * n)
        slot = own_ids[jnp.clip(number, 0, 8 * n - 1)] - first_id
        slot = jnp.where(valid, slot, -1000)
        held = [jnp.where(low_lane == slot - 8 * w, number, held[w]) for w in range(3)]
    near = near_ids[...]
    found = [jnp.zeros((8, 128), jnp.bool_) for _ in range(3)]
    for j in range(16):
        column = jnp.broadcast_to(near[:, j : j + 1], (8, 128))
        found = [found[w] | (column == held[w]) for w in range(3)]
    masks = [jnp.where(found[w] | (low_lane >= 8), 0.0, MASKED) for w in range(3)]
    mask_out[0] = masks[2]
    mask_out[1] = masks[0]
    start(lambda flow: [mask_copy(flow)])
    for chunk in range(1, AHEAD):
        start(bulk_copies(jnp.int32(chunk)))

    def spread(block, mask):
        for a in range(8):
            rows = pl.ds(ROWS * block + 64 * a, 64)
            bias[rows, :] = jnp.broadcast_to(mask[a : a + 1, :], (64, 128)).astype(BF16)

    spread(1, masks[1])
    row_slot = lax.broadcasted_iota(jnp.int32, (ROWS, 128), 0) // 64
    lane_slot = lax.rem(lax.broadcasted_iota(jnp.int32, (ROWS, 128), 1), 64)
    hot[...] = jnp.where(row_slot == lane_slot, 1.0, 0.0).astype(BF16)

    for flow in (0, 1):

        @pl.when(jnp.logical_not(receives[flow]))
        def _(flow=flow):
            rows = pl.ds(2 * ROWS * flow, ROWS)
            for pair in range(PAIRS):
                q_all[pair, rows, :] = jnp.zeros((ROWS, 128), BF16)
                g_all[pair, rows, :] = jnp.zeros((ROWS, 128), BF16)
            mask_in[flow] = jnp.full((8, 128), MASKED, F32)
            stat_in[flow] = jnp.full((CHUNKS, 2, 8, 128), MASKED, F32)
            dq_in[flow] = jnp.zeros((CHUNKS, 2, 64, TILE), BF16)

        @pl.when(jnp.logical_not(far_receives[flow]))
        def _(flow=flow):
            stat_far[flow] = jnp.full((CHUNKS, 8, 128), MASKED, F32)

    for pair in range(PAIRS):
        for array in range(4):
            load(pair, array).wait()
    for pair in range(PAIRS):
        k_turned[pair] = k_pair[pair].T

    half = lax.broadcasted_iota(jnp.int32, (1, 128), 1) < 64
    halves = (half, jnp.logical_not(half))

    def keys_of(pair, h):
        return (
            jnp.where(halves[h], k_pair[pair], hot[...]),
            jnp.where(halves[h], v_pair[pair], jnp.zeros((), BF16)),
        )

    def scores_of(keys, values, pair, rows, h, e_ref, d_ref):
        queries = jnp.where(halves[h], q_all[pair, rows, :], bias[rows, :])
        scores = dot_last(keys, queries)
        peak = jnp.max(scores, axis=0, keepdims=True)
        raised = jnp.exp2((scores - peak) * base2)
        e_ref[...] = raised
        dweights = dot_last(values, g_all[pair, rows, :])
        d_ref[...] = dweights
        total = jnp.sum(raised, axis=0, keepdims=True)
        weighted = jnp.sum(raised * dweights, axis=0, keepdims=True)
        raised_by = peak * base2
        return raised_by, raised_by + jnp.log2(total), weighted / total

    def packed(found):
        rows = [row for peak, log_total, delta in found for row in halved(log_total)]
        rows += [row for peak, log_total, delta in found for row in halved(delta)]
        return jnp.concatenate(rows, axis=0)

    def halved(row):
        return [row[:, :128], row[:, 128:]]

    def keep_peaks(block, chunk, found):
        for h in (0, 1):
            peaks[block, chunk, h : h + 1, :] = found[h][0]

    def own_scores(pair, carry):
        both = [keys_of(pair, h) for h in (0, 1)]
        for t in (0, 1):
            chunk = 2 * pair + t
            found = []
            for h in (0, 1):
                rows = pl.ds(ROWS + TILE * t, TILE)
                found += [
                    scores_of(*both[h], pair, rows, h, e_own.at[chunk, h], d_own.at[chunk, h])
                ]
            keep_peaks(1, chunk, found)
            stat_out[0, chunk, 0] = packed(found)
            stat_out[1, chunk, 0] = packed(found)
        return carry

    lax.fori_loop(0, PAIRS, own_scores, 0)

    wait_recv(lambda flow: [mask_copy(flow)])
    spread(0, mask_in[0])
    spread(2, mask_in[1])

    def near_scores(chunk):
        pair, first = split(chunk)
        slot = lax.rem(chunk, RING)
        found = [[], []]
        for h in (0, 1):
            keys, values = keys_of(pair, h)
            for side in (0, 1):
                rows = pl.ds(2 * ROWS * side + first, TILE)
                e_ref, d_ref = e_near.at[slot, side, h], d_near.at[slot, side, h]
                found[side] += [scores_of(keys, values, pair, rows, h, e_ref, d_ref)]
        for side in (0, 1):
            keep_peaks(2 * side, chunk, found[side])
            stat_out[1 - side, chunk, 1] = packed(found[side])

    def combined(parts):
        logs, deltas = [part[:4] for part in parts], [part[4:] for part in parts]
        top = functools.reduce(jnp.maximum, logs)
        scales = [jnp.exp2(one - top) for one in logs]
        total = sum(scales)
        delta = sum(scale * one for scale, one in zip(scales, deltas)) / total
        return top + jnp.log2(total), delta

    def finish(chunk):
        pair, first = split(chunk)
        slot = lax.rem(chunk, RING)
        finals = [
            combined([stat_out[1, chunk, 1], stat_in[0, chunk, 0], stat_far[0, chunk]]),
            combined([stat_out[0, chunk, 0], stat_in[0, chunk, 1], stat_in[1, chunk, 1]]),
            combined([stat_out[0, chunk, 1], stat_in[1, chunk, 0], stat_far[1, chunk]]),
        ]

        def one(h, block):
            side = block // 2
            if block == 1:
                e_ref, d_ref = e_own.at[chunk, h], d_own.at[chunk, h]
            else:
                e_ref, d_ref = e_near.at[slot, side, h], d_near.at[slot, side, h]
            log_total, delta = (
                jnp.concatenate([one[2 * h : 2 * h + 1], one[2 * h + 1 : 2 * h + 2]], axis=1)
                for one in finals[block]
            )
            weight = e_ref[...] * jnp.exp2(peaks[block, chunk, h : h + 1, :] - log_total)
            dscore = (weight * (d_ref[...] - delta)).astype(BF16)
            lanes = pl.ds(ROWS * block + first, TILE)
            weights[h, :, lanes] = weight.astype(BF16)
            dscores[h, :, lanes] = dscore
            part = dot(k_turned[pair, pl.ds(64 * h, 64), :], dscore)
            if block == 1:
                dq_own[chunk, pl.ds(64 * h, 64), :] = part
            else:
                dq_out[1 - side, chunk, h] = part.astype(BF16)

        for h in (0, 1):
            one(h, 0)
            one(h, 2)

            @pl.when(chunk >= 1)
            def _(h=h):
                start(lambda flow: [dq_copy(chunk, flow, h)])

        @pl.when(chunk == 1)
        def _():
            start(lambda flow: [dq_copy(0, flow, h) for h in (0, 1)])

        for h in (0, 1):
            one(h, 1)

    def key_gradients(pair):
        dv = [dot(weights[h], g_all[pair]) for h in (0, 1)]
        dk = [dot(dscores[h], q_all[pair]) for h in (0, 1)]
        grad_value[pair] = jnp.where(half, dv[0], dv[1]).astype(BF16)
        grad_key[pair] = (jnp.where(half, dk[0], dk[1]) * scaling).astype(BF16)

    def query_gradients(chunk):
        near = [dq_in[flow, chunk].reshape(128, TILE).astype(F32) for flow in (0, 1)]
        total = dq_own[chunk] + near[0] + near[1]
        grad_query[chunk] = (total * scaling).T.astype(BF16)

    def step(s, carry):
        @pl.when(s < CHUNKS)
        def _():
            wait_recv(bulk_copies(s))
            near_scores(s)
            start(lambda flow: [stat_copy(s, flow)])
            start(lambda flow: [far_copy(s, flow)], far_sends)

            @pl.when(s + AHEAD < CHUNKS)
            def _():
                start(bulk_copies(s + AHEAD))

        @pl.when((s >= LAG_C) & (s < CHUNKS + LAG_C))
        def _():
            chunk = s - LAG_C
            wait_recv(lambda flow: [stat_copy(chunk, flow)])
            wait_recv(lambda flow: [far_copy(chunk, flow)], far_receives)
            finish(chunk)

            @pl.when(lax.rem(chunk, 2) == 1)
            def _():
                key_gradients(lax.div(chunk, 2))

        @pl.when(s >= LAG_D)
        def _():
            sum_queries(s - LAG_D)

        return carry

    def sum_queries(chunk):
        wait_recv(lambda flow: [dq_copy(chunk, flow, h) for h in (0, 1)])
        query_gradients(chunk)

    lax.fori_loop(0, CHUNKS + LAG_D - 1, step, 0)

    wait_send(lambda flow: [mask_copy(flow)])

    def drain(chunk, carry):
        wait_send(
            lambda flow: [
                *bulk_copies(chunk)(flow),
                stat_copy(chunk, flow),
                dq_copy(chunk, flow, 0),
                dq_copy(chunk, flow, 1),
            ]
        )
        wait_send(lambda flow: [far_copy(chunk, flow)], far_sends)
        return carry

    lax.fori_loop(0, CHUNKS, drain, 0)
    sum_queries(CHUNKS - 1)


def write_out(dq, dk, dv, grad_query, grad_key, grad_value, sem):
    copies = []
    for chunk in range(CHUNKS):
        place = (pl.ds(TILE * (chunk % 2), TILE), pl.ds(128 * (chunk // 2), 128))
        copies.append((dq.at[chunk], grad_query.at[place]))
    for pair in range(PAIRS):
        place = (slice(None), pl.ds(128 * pair, 128))
        copies.append((dk.at[pair], grad_key.at[place]))
        copies.append((dv.at[pair], grad_value.at[place]))
    copies = [pltpu.make_async_copy(*one, sem.at[i]) for i, one in enumerate(copies)]
    for copy in copies:
        copy.start()
    for copy in copies:
        copy.wait()


def body(n, query_rows, key_rows, value_rows, grad_output, neighbours, owner):
    rows, features = query_rows.shape
    out = jax.ShapeDtypeStruct((rows, features), BF16)
    far, near = pl.BlockSpec(memory_space=pl.ANY), pl.BlockSpec(memory_space=pltpu.VMEM)
    dma = pltpu.SemaphoreType.DMA
    wide = ROWS * 3
    parts = pl.pallas_call(
        functools.partial(kernel, n),
        out_shape=[
            pltpu.VMEM((CHUNKS, TILE, 128), BF16),
            pltpu.VMEM((PAIRS, ROWS, 128), BF16),
            pltpu.VMEM((PAIRS, ROWS, 128), BF16),
        ],
        in_specs=[far] * 6,
        out_specs=[near] * 3,
        scratch_shapes=[
            pltpu.SMEM(owner.shape, jnp.int32),
            pltpu.VMEM(neighbours.shape, jnp.int32),
            pltpu.VMEM((PAIRS, ROWS, 128), BF16),
            pltpu.VMEM((PAIRS, ROWS, 128), BF16),
            pltpu.VMEM((PAIRS, 128, ROWS), BF16),
            pltpu.VMEM((PAIRS, wide, 128), BF16),
            pltpu.VMEM((PAIRS, wide, 128), BF16),
            pltpu.VMEM((wide, 128), BF16),
            pltpu.VMEM((ROWS, 128), BF16),
            pltpu.VMEM((2, 8, 128), F32),
            pltpu.VMEM((2, 8, 128), F32),
            pltpu.VMEM((CHUNKS, 2, ROWS, TILE), F32),
            pltpu.VMEM((CHUNKS, 2, ROWS, TILE), F32),
            pltpu.VMEM((RING, 2, 2, ROWS, TILE), F32),
            pltpu.VMEM((RING, 2, 2, ROWS, TILE), F32),
            pltpu.VMEM((3, CHUNKS, 8, TILE), F32),
            pltpu.VMEM((2, CHUNKS, 2, 8, 128), F32),
            pltpu.VMEM((2, CHUNKS, 2, 8, 128), F32),
            pltpu.VMEM((2, CHUNKS, 8, 128), F32),
            pltpu.VMEM((2, ROWS, wide), BF16),
            pltpu.VMEM((2, ROWS, wide), BF16),
            pltpu.VMEM((CHUNKS, 128, TILE), F32),
            pltpu.VMEM((2, CHUNKS, 2, 64, TILE), BF16),
            pltpu.VMEM((2, CHUNKS, 2, 64, TILE), BF16),
            dma((4 * PAIRS + 2,)),
            dma((2, CHUNKS, 2)),
            dma((2, CHUNKS, 2)),
            dma((2,)),
            dma((2,)),
            dma((2, CHUNKS)),
            dma((2, CHUNKS)),
            dma((2, CHUNKS)),
            dma((2, CHUNKS)),
            dma((2, CHUNKS, 2)),
            dma((2, CHUNKS, 2)),
        ],
        compiler_params=pltpu.CompilerParams(
            collective_id=0, has_side_effects=True, vmem_limit_bytes=58 << 20
        ),
    )(query_rows, key_rows, value_rows, grad_output, neighbours, owner)
    return pl.pallas_call(
        write_out,
        out_shape=[out] * 3,
        in_specs=[near] * 3,
        out_specs=[far] * 3,
        scratch_shapes=[dma((CHUNKS + 2 * PAIRS,))],
    )(*[pltpu.with_memory_space_constraint(one, pltpu.VMEM) for one in parts])


def solution(mesh):
    split = P(("scene", "patch"), None)
    return jax.shard_map(
        functools.partial(body, mesh.shape["patch"]),
        mesh=mesh,
        in_specs=(split, split, split, split, split, P("scene")),
        out_specs=(split, split, split),
        check_vma=False,
    )
```

```python
import functools
import math

import jax
import jax.numpy as jnp
from jax import lax
from jax.experimental import pallas as pl
from jax.experimental.pallas import tpu as pltpu
from jax.sharding import PartitionSpec as P

HEADS = 8
MESH = pl.DeviceIdType.MESH
BF16, F32 = jnp.bfloat16, jnp.float32
MASKED = -1e30
ROWS = 512
TILE = 256
PAIRS = 4
CHUNKS = PAIRS * ROWS // TILE
RING = 4
LAG_C, LAG_D = 3, 7
AHEAD = 3


def dot(left, right):
    return lax.dot_general(left, right, (((1,), (0,)), ((), ())), preferred_element_type=F32)


def dot_last(left, right):
    return lax.dot_general(left, right, (((1,), (1,)), ((), ())), preferred_element_type=F32)


def kernel(
    n,
    query, key, value, gout, neighbours, owner,
    grad_query, grad_key, grad_value,
    own_ids, near_ids, k_pair, v_pair, k_turned, rows_all, bias, hot, mask_out, mask_in,
    e_own, d_own, e_near, d_near, peaks, stat_out, stat_in,
    weights, dscores, dq_own, dq_out, dq_in,
    load_sem, bulk_send, bulk_recv, mask_send, mask_recv, stat_send, stat_recv, far_send, dq_send,
):
    me = lax.axis_index("patch")
    target = (jnp.minimum(me + 1, n - 1), jnp.maximum(me - 1, 0))
    sends = (me < n - 1, me > 0)
    receives = (me > 0, me < n - 1)
    far_target = (jnp.minimum(me + 2, n - 1), jnp.maximum(me - 2, 0))
    far_sends = (me < n - 2, me > 1)
    far_receives = (me > 1, me < n - 2)
    scaling = 1.0 / math.sqrt(64)
    base2 = scaling * math.log2(math.e)

    barrier = pltpu.get_barrier_semaphore()
    peers = jnp.int32(0)
    for exists, peer in zip(sends + far_sends, target + far_target):
        peers = peers + exists.astype(jnp.int32)

        @pl.when(exists)
        def _(peer=peer):
            pl.semaphore_signal(barrier, inc=1, device_id={"patch": peer}, device_id_type=MESH)

    own_copy = pltpu.make_async_copy(owner, own_ids, load_sem.at[4])
    near_copy = pltpu.make_async_copy(neighbours, near_ids, load_sem.at[5])
    own_copy.start()
    near_copy.start()

    def load(pair, array):
        lanes = pl.ds(128 * pair, 128)
        middle = pl.ds(ROWS, ROWS)
        source = (key, value, query, gout)[array].at[:, lanes]
        place = (
            k_pair.at[pair],
            v_pair.at[pair],
            rows_all.at[pair, 0, middle],
            rows_all.at[pair, 1, middle],
        )[array]
        return pltpu.make_async_copy(source, place, load_sem.at[array])

    pl.semaphore_wait(barrier, peers)

    def remote(source, place, send_sem, recv_sem, flow):
        return pltpu.make_async_remote_copy(
            src_ref=source,
            dst_ref=place,
            send_sem=send_sem,
            recv_sem=recv_sem,
            device_id={"patch": target[flow]},
            device_id_type=MESH,
        )

    def mask_copy(flow):
        return remote(
            mask_out.at[flow], mask_in.at[flow], mask_send.at[flow], mask_recv.at[flow], flow
        )

    def split(chunk):
        pair = lax.div(chunk, 2)
        first = pl.multiple_of(lax.rem(chunk, 2) * TILE, TILE)
        return pair, first

    def bulk_copy(chunk, flow, array):
        pair, first = split(chunk)
        lanes = pl.ds(pl.multiple_of(pair * 128, 128), 128)
        source = (query, gout)[array].at[pl.ds(first, TILE), lanes]
        place = rows_all.at[pair, array, pl.ds(2 * ROWS * flow + first, TILE)]
        return remote(source, place, bulk_send.at[flow], bulk_recv.at[flow, chunk], flow)

    def whole(place, send_sem, recv_sem, flow):
        return remote(place, place, send_sem, recv_sem, flow)

    def bulk_arrival(chunk, flow):
        pair, first = split(chunk)
        place = rows_all.at[pair, :, pl.ds(2 * ROWS * flow + first, TILE)]
        return whole(place, bulk_send.at[flow], bulk_recv.at[flow, chunk], flow)

    def stat_copy(chunk, flow):
        place = stat_in.at[flow, chunk, pl.ds(0, 2)]
        at = (flow, chunk)
        return remote(stat_out.at[at], place, stat_send.at[flow], stat_recv.at[at], flow)

    def far_copy(chunk, flow):
        return pltpu.make_async_remote_copy(
            src_ref=stat_out.at[flow, chunk, 1],
            dst_ref=stat_in.at[flow, chunk, 2],
            send_sem=far_send.at[flow],
            recv_sem=stat_recv.at[flow, chunk],
            device_id={"patch": far_target[flow]},
            device_id_type=MESH,
        )

    def wait_stats(chunk):
        for flow in (0, 1):

            @pl.when(far_receives[flow])
            def _(flow=flow):
                at = (flow, chunk)
                whole(stat_in.at[at], stat_send.at[flow], stat_recv.at[at], flow).wait_recv()

            @pl.when(receives[flow] & jnp.logical_not(far_receives[flow]))
            def _(flow=flow):
                stat_copy(chunk, flow).wait_recv()

    def dq_copy(chunk, flow, h):
        at = (flow, chunk)
        source, place = (ref.at[flow, chunk, h] for ref in (dq_out, dq_in))
        return remote(source, place, dq_send.at[flow], bulk_recv.at[at], flow)

    def dq_arrival(chunk, flow):
        at = (flow, chunk)
        return whole(dq_in.at[at], dq_send.at[flow], bulk_recv.at[at], flow)

    def start(copies, when=sends):
        for flow in (0, 1):

            @pl.when(when[flow])
            def _(flow=flow):
                for copy in copies(flow):
                    copy.start()

    def wait_send(copies, when=sends):
        for flow in (0, 1):

            @pl.when(when[flow])
            def _(flow=flow):
                for copy in copies(flow):
                    copy.wait_send()

    def wait_recv(copies, when=receives):
        for flow in (0, 1):

            @pl.when(when[flow])
            def _(flow=flow):
                for copy in copies(flow):
                    copy.wait_recv()

    def bulk_copies(chunk):
        return lambda flow: [bulk_copy(chunk, flow, array) for array in (0, 1)]

    start(bulk_copies(jnp.int32(0)))

    for pair in range(PAIRS):
        for array in range(4):
            load(pair, array).start()

    own_copy.wait()
    near_copy.wait()
    lane = lax.broadcasted_iota(jnp.int32, (8, 128), 1)
    low_lane = lax.rem(lane, 64)
    first_id = 8 * (me - 1)
    held = [jnp.full((8, 128), -1, jnp.int32) for _ in range(3)]
    for t in range(24):
        number = first_id + t
        valid = (number >= 0) & (number < 8 * n)
        slot = own_ids[jnp.clip(number, 0, 8 * n - 1)] - first_id
        slot = jnp.where(valid, slot, -1000)
        held = [jnp.where(low_lane == slot - 8 * w, number, held[w]) for w in range(3)]
    near = near_ids[...]
    found = [jnp.zeros((8, 128), jnp.bool_) for _ in range(3)]
    for j in range(16):
        column = jnp.broadcast_to(near[:, j : j + 1], (8, 128))
        found = [found[w] | (column == held[w]) for w in range(3)]
    masks = [jnp.where(found[w] | (low_lane >= 8), 0.0, MASKED) for w in range(3)]
    mask_out[0] = masks[2]
    mask_out[1] = masks[0]
    start(lambda flow: [mask_copy(flow)])
    for chunk in range(1, AHEAD):
        start(bulk_copies(jnp.int32(chunk)))

    def spread(block, mask):
        for a in range(8):
            rows = pl.ds(ROWS * block + 64 * a, 64)
            bias[rows, :] = jnp.broadcast_to(mask[a : a + 1, :], (64, 128)).astype(BF16)

    spread(1, masks[1])
    row_slot = lax.broadcasted_iota(jnp.int32, (ROWS, 128), 0) // 64
    lane_slot = lax.rem(lax.broadcasted_iota(jnp.int32, (ROWS, 128), 1), 64)
    hot[...] = jnp.where(row_slot == lane_slot, 1.0, 0.0).astype(BF16)

    for flow in (0, 1):

        @pl.when(jnp.logical_not(receives[flow]))
        def _(flow=flow):
            rows = pl.ds(2 * ROWS * flow, ROWS)
            for pair in range(PAIRS):
                rows_all[pair, :, rows, :] = jnp.zeros((2, ROWS, 128), BF16)
            mask_in[flow] = jnp.full((8, 128), MASKED, F32)
            stat_in[flow, :, 0:2] = jnp.full((CHUNKS, 2, 8, 128), MASKED, F32)
            dq_in[flow] = jnp.zeros((CHUNKS, 2, 64, TILE), BF16)

        @pl.when(jnp.logical_not(far_receives[flow]))
        def _(flow=flow):
            stat_in[flow, :, 2] = jnp.full((CHUNKS, 8, 128), MASKED, F32)

    middle = pl.ds(ROWS, ROWS)
    places = (k_pair, v_pair, rows_all.at[:, 0, middle], rows_all.at[:, 1, middle])
    for array, place in enumerate(places):
        pltpu.make_async_copy(place, place, load_sem.at[array]).wait()
    for pair in range(PAIRS):
        k_turned[pair] = k_pair[pair].T

    half = lax.broadcasted_iota(jnp.int32, (1, 128), 1) < 64
    halves = (half, jnp.logical_not(half))

    def keys_of(pair, h):
        return (
            jnp.where(halves[h], k_pair[pair], hot[...]),
            jnp.where(halves[h], v_pair[pair], jnp.zeros((), BF16)),
        )

    def scores_of(keys, values, pair, rows, h, e_ref, d_ref):
        queries = jnp.where(halves[h], rows_all[pair, 0, rows, :], bias[rows, :])
        scores = dot_last(keys, queries)
        peak = jnp.max(scores, axis=0, keepdims=True)
        raised = jnp.exp2((scores - peak) * base2)
        e_ref[...] = raised
        dweights = dot_last(values, rows_all[pair, 1, rows, :])
        d_ref[...] = dweights
        total = jnp.sum(raised, axis=0, keepdims=True)
        weighted = jnp.sum(raised * dweights, axis=0, keepdims=True)
        raised_by = peak * base2
        return raised_by, raised_by + jnp.log2(total), weighted / total

    def packed(found):
        rows = [row for peak, log_total, delta in found for row in halved(log_total)]
        rows += [row for peak, log_total, delta in found for row in halved(delta)]
        return jnp.concatenate(rows, axis=0)

    def halved(row):
        return [row[:, :128], row[:, 128:]]

    def keep_peaks(block, chunk, found):
        for h in (0, 1):
            peaks[block, chunk, h : h + 1, :] = found[h][0]

    def own_scores(pair, carry):
        both = [keys_of(pair, h) for h in (0, 1)]
        for t in (0, 1):
            chunk = 2 * pair + t
            found = []
            for h in (0, 1):
                rows = pl.ds(ROWS + TILE * t, TILE)
                found += [
                    scores_of(*both[h], pair, rows, h, e_own.at[chunk, h], d_own.at[chunk, h])
                ]
            keep_peaks(1, chunk, found)
            stat_out[0, chunk, 0] = packed(found)
            stat_out[1, chunk, 0] = packed(found)
        return carry

    lax.fori_loop(0, PAIRS, own_scores, 0)

    wait_recv(lambda flow: [mask_copy(flow)])
    spread(0, mask_in[0])
    spread(2, mask_in[1])

    def near_scores(chunk):
        pair, first = split(chunk)
        slot = lax.rem(chunk, RING)
        found = [[], []]
        for h in (0, 1):
            keys, values = keys_of(pair, h)
            for side in (0, 1):
                rows = pl.ds(2 * ROWS * side + first, TILE)
                e_ref, d_ref = e_near.at[slot, side, h], d_near.at[slot, side, h]
                found[side] += [scores_of(keys, values, pair, rows, h, e_ref, d_ref)]
        for side in (0, 1):
            keep_peaks(2 * side, chunk, found[side])
            stat_out[1 - side, chunk, 1] = packed(found[side])

    def combined(parts):
        logs, deltas = [part[:4] for part in parts], [part[4:] for part in parts]
        top = functools.reduce(jnp.maximum, logs)
        scales = [jnp.exp2(one - top) for one in logs]
        total = sum(scales)
        delta = sum(scale * one for scale, one in zip(scales, deltas)) / total
        return top + jnp.log2(total), delta

    def finish(chunk):
        pair, first = split(chunk)
        slot = lax.rem(chunk, RING)
        finals = [
            combined([stat_out[1, chunk, 1], stat_in[0, chunk, 0], stat_in[0, chunk, 2]]),
            combined([stat_out[0, chunk, 0], stat_in[0, chunk, 1], stat_in[1, chunk, 1]]),
            combined([stat_out[0, chunk, 1], stat_in[1, chunk, 0], stat_in[1, chunk, 2]]),
        ]

        def one(h, block):
            side = block // 2
            if block == 1:
                e_ref, d_ref = e_own.at[chunk, h], d_own.at[chunk, h]
            else:
                e_ref, d_ref = e_near.at[slot, side, h], d_near.at[slot, side, h]
            log_total, delta = (
                jnp.concatenate([one[2 * h : 2 * h + 1], one[2 * h + 1 : 2 * h + 2]], axis=1)
                for one in finals[block]
            )
            weight = e_ref[...] * jnp.exp2(peaks[block, chunk, h : h + 1, :] - log_total)
            dscore = (weight * (d_ref[...] - delta)).astype(BF16)
            lanes = pl.ds(ROWS * block + first, TILE)
            rows = pl.ds(ROWS * h, ROWS)
            weights[rows, lanes] = weight.astype(BF16)
            dscores[rows, lanes] = dscore
            part = dot(k_turned[pair, pl.ds(64 * h, 64), :], dscore)
            if block == 1:
                dq_own[chunk, pl.ds(64 * h, 64), :] = part
            else:
                dq_out[1 - side, chunk, h] = part.astype(BF16)

        for h in (0, 1):
            one(h, 0)
            one(h, 2)

            @pl.when(chunk >= 1)
            def _(h=h):
                start(lambda flow: [dq_copy(chunk, flow, h)])

        @pl.when(chunk == 1)
        def _():
            start(lambda flow: [dq_copy(0, flow, h) for h in (0, 1)])

        for h in (0, 1):
            one(h, 1)

    def key_gradients(pair):
        dv = dot(weights[...], rows_all[pair, 1])
        dk = dot(dscores[...], rows_all[pair, 0])
        lanes = pl.ds(pl.multiple_of(pair * 128, 128), 128)
        grad_value[:, lanes] = jnp.where(half, dv[:ROWS], dv[ROWS:]).astype(BF16)
        grad_key[:, lanes] = (jnp.where(half, dk[:ROWS], dk[ROWS:]) * scaling).astype(BF16)

    def query_gradients(chunk):
        near = [dq_in[flow, chunk].reshape(128, TILE).astype(F32) for flow in (0, 1)]
        total = dq_own[chunk] + near[0] + near[1]
        pair, first = split(chunk)
        lanes = pl.ds(pl.multiple_of(pair * 128, 128), 128)
        grad_query[pl.ds(first, TILE), lanes] = (total * scaling).T.astype(BF16)

    def step(s, carry):
        @pl.when(s < CHUNKS)
        def _():
            wait_recv(lambda flow: [bulk_arrival(s, flow)])
            near_scores(s)
            start(lambda flow: [stat_copy(s, flow)])
            start(lambda flow: [far_copy(s, flow)], far_sends)

            @pl.when(s + AHEAD < CHUNKS)
            def _():
                start(bulk_copies(s + AHEAD))

        @pl.when((s >= LAG_C) & (s < CHUNKS + LAG_C))
        def _():
            chunk = s - LAG_C
            wait_stats(chunk)
            finish(chunk)

            @pl.when(lax.rem(chunk, 2) == 1)
            def _():
                key_gradients(lax.div(chunk, 2))

        @pl.when(s >= LAG_D)
        def _():
            sum_queries(s - LAG_D)

        return carry

    def sum_queries(chunk):
        wait_recv(lambda flow: [dq_arrival(chunk, flow)])
        query_gradients(chunk)

    lax.fori_loop(0, CHUNKS + LAG_D - 1, step, 0)

    wait_send(
        lambda flow: [
            mask_copy(flow),
            whole(rows_all.at[:, :, middle], bulk_send.at[flow], bulk_recv.at[flow, 0], flow),
            whole(stat_out.at[flow], stat_send.at[flow], stat_recv.at[flow, 0], flow),
            whole(dq_out.at[flow], dq_send.at[flow], bulk_recv.at[flow, 0], flow),
        ]
    )
    wait_send(
        lambda flow: [
            whole(stat_out.at[flow, :, 1], far_send.at[flow], stat_recv.at[flow, 0], flow)
        ],
        far_sends,
    )
    sum_queries(CHUNKS - 1)


def write_out(*refs):
    sources, places, sem = refs[:3], refs[3:6], refs[6]
    copies = [
        pltpu.make_async_copy(source, place, sem.at[i])
        for i, (source, place) in enumerate(zip(sources, places))
    ]
    for copy in copies:
        copy.start()
    for copy in copies:
        copy.wait()


def body(n, query_rows, key_rows, value_rows, grad_output, neighbours, owner):
    rows, features = query_rows.shape
    out = jax.ShapeDtypeStruct((rows, features), BF16)
    far, near = pl.BlockSpec(memory_space=pl.ANY), pl.BlockSpec(memory_space=pltpu.VMEM)
    dma = pltpu.SemaphoreType.DMA
    wide = ROWS * 3
    parts = pl.pallas_call(
        functools.partial(kernel, n),
        out_shape=[pltpu.VMEM((rows, features), BF16)] * 3,
        in_specs=[far] * 6,
        out_specs=[near] * 3,
        scratch_shapes=[
            pltpu.SMEM(owner.shape, jnp.int32),
            pltpu.VMEM(neighbours.shape, jnp.int32),
            pltpu.VMEM((PAIRS, ROWS, 128), BF16),
            pltpu.VMEM((PAIRS, ROWS, 128), BF16),
            pltpu.VMEM((PAIRS, 128, ROWS), BF16),
            pltpu.VMEM((PAIRS, 2, wide, 128), BF16),
            pltpu.VMEM((wide, 128), BF16),
            pltpu.VMEM((ROWS, 128), BF16),
            pltpu.VMEM((2, 8, 128), F32),
            pltpu.VMEM((2, 8, 128), F32),
            pltpu.VMEM((CHUNKS, 2, ROWS, TILE), F32),
            pltpu.VMEM((CHUNKS, 2, ROWS, TILE), F32),
            pltpu.VMEM((RING, 2, 2, ROWS, TILE), F32),
            pltpu.VMEM((RING, 2, 2, ROWS, TILE), F32),
            pltpu.VMEM((3, CHUNKS, 8, TILE), F32),
            pltpu.VMEM((2, CHUNKS, 2, 8, 128), F32),
            pltpu.VMEM((2, CHUNKS, 3, 8, 128), F32),
            pltpu.VMEM((2 * ROWS, wide), BF16),
            pltpu.VMEM((2 * ROWS, wide), BF16),
            pltpu.VMEM((CHUNKS, 128, TILE), F32),
            pltpu.VMEM((2, CHUNKS, 2, 64, TILE), BF16),
            pltpu.VMEM((2, CHUNKS, 2, 64, TILE), BF16),
            dma((6,)),
            dma((2,)),
            dma((2, CHUNKS)),
            dma((2,)),
            dma((2,)),
            dma((2,)),
            dma((2, CHUNKS)),
            dma((2,)),
            dma((2,)),
        ],
        compiler_params=pltpu.CompilerParams(
            collective_id=0, has_side_effects=True, vmem_limit_bytes=58 << 20
        ),
    )(query_rows, key_rows, value_rows, grad_output, neighbours, owner)
    return pl.pallas_call(
        write_out,
        out_shape=[out] * 3,
        in_specs=[near] * 3,
        out_specs=[far] * 3,
        scratch_shapes=[dma((3,))],
    )(*[pltpu.with_memory_space_constraint(one, pltpu.VMEM) for one in parts])


def solution(mesh):
    split = P(("scene", "patch"), None)
    return jax.shard_map(
        functools.partial(body, mesh.shape["patch"]),
        mesh=mesh,
        in_specs=(split, split, split, split, split, P("scene")),
        out_specs=(split, split, split),
        check_vma=False,
    )
```

```python
import functools
import math

import jax
import jax.numpy as jnp
from jax import lax
from jax.experimental import pallas as pl
from jax.experimental.pallas import tpu as pltpu
from jax.sharding import PartitionSpec as P

HEADS = 8
MESH = pl.DeviceIdType.MESH
BF16, F32 = jnp.bfloat16, jnp.float32
MASKED = -1e30
ROWS = 512
TILE = 256
PAIRS = 4
CHUNKS = PAIRS * ROWS // TILE
RING = 4
LAG_C, LAG_D = 3, 8
AHEAD = 3


def dot(left, right):
    return lax.dot_general(left, right, (((1,), (0,)), ((), ())), preferred_element_type=F32)


def dot_last(left, right):
    return lax.dot_general(left, right, (((1,), (1,)), ((), ())), preferred_element_type=F32)


def kernel(
    n,
    query, key, value, gout, neighbours, owner,
    grad_query, grad_key, grad_value,
    own_ids, near_ids, k_pair, v_pair, k_turned, rows_all, bias, hot, mask_out, mask_in,
    e_own, d_own, e_near, d_near, peaks, stat_out, stat_in,
    weights, dscores, dq_own, dq_out, dq_in,
    load_sem, bulk_send, bulk_recv, mask_send, mask_recv, stat_send, stat_recv, far_send, dq_send,
):
    me = lax.axis_index("patch")
    target = (jnp.minimum(me + 1, n - 1), jnp.maximum(me - 1, 0))
    sends = (me < n - 1, me > 0)
    receives = (me > 0, me < n - 1)
    far_target = (jnp.minimum(me + 2, n - 1), jnp.maximum(me - 2, 0))
    far_sends = (me < n - 2, me > 1)
    far_receives = (me > 1, me < n - 2)
    scaling = 1.0 / math.sqrt(64)
    base2 = scaling * math.log2(math.e)

    barrier = pltpu.get_barrier_semaphore()
    peers = jnp.int32(0)
    for exists, peer in zip(sends + far_sends, target + far_target):
        peers = peers + exists.astype(jnp.int32)

        @pl.when(exists)
        def _(peer=peer):
            pl.semaphore_signal(barrier, inc=1, device_id={"patch": peer}, device_id_type=MESH)

    own_copy = pltpu.make_async_copy(owner, own_ids, load_sem.at[4])
    near_copy = pltpu.make_async_copy(neighbours, near_ids, load_sem.at[5])
    own_copy.start()
    near_copy.start()

    def load(pair, array):
        lanes = pl.ds(128 * pair, 128)
        middle = pl.ds(ROWS, ROWS)
        source = (key, value, query, gout)[array].at[:, lanes]
        place = (
            k_pair.at[pair],
            v_pair.at[pair],
            rows_all.at[pair, 0, middle],
            rows_all.at[pair, 1, middle],
        )[array]
        return pltpu.make_async_copy(source, place, load_sem.at[array])

    pl.semaphore_wait(barrier, peers)

    def remote(source, place, send_sem, recv_sem, flow):
        return pltpu.make_async_remote_copy(
            src_ref=source,
            dst_ref=place,
            send_sem=send_sem,
            recv_sem=recv_sem,
            device_id={"patch": target[flow]},
            device_id_type=MESH,
        )

    def mask_copy(flow):
        return remote(
            mask_out.at[flow], mask_in.at[flow], mask_send.at[flow], mask_recv.at[flow], flow
        )

    def split(chunk):
        pair = lax.div(chunk, 2)
        first = pl.multiple_of(lax.rem(chunk, 2) * TILE, TILE)
        return pair, first

    def bulk_copy(chunk, flow, array):
        pair, first = split(chunk)
        lanes = pl.ds(pl.multiple_of(pair * 128, 128), 128)
        source = (query, gout)[array].at[pl.ds(first, TILE), lanes]
        place = rows_all.at[pair, array, pl.ds(2 * ROWS * flow + first, TILE)]
        return remote(source, place, bulk_send.at[flow], bulk_recv.at[flow, chunk], flow)

    def whole(place, send_sem, recv_sem, flow):
        return remote(place, place, send_sem, recv_sem, flow)

    def bulk_arrival(chunk, flow):
        pair, first = split(chunk)
        place = rows_all.at[pair, :, pl.ds(2 * ROWS * flow + first, TILE)]
        return whole(place, bulk_send.at[flow], bulk_recv.at[flow, chunk], flow)

    def stat_copy(chunk, flow):
        place = stat_in.at[flow, chunk, pl.ds(0, 2)]
        at = (flow, chunk)
        return remote(stat_out.at[at], place, stat_send.at[flow], stat_recv.at[at], flow)

    def far_copy(chunk, flow):
        return pltpu.make_async_remote_copy(
            src_ref=stat_out.at[flow, chunk, 1],
            dst_ref=stat_in.at[flow, chunk, 2],
            send_sem=far_send.at[flow],
            recv_sem=stat_recv.at[flow, chunk],
            device_id={"patch": far_target[flow]},
            device_id_type=MESH,
        )

    def wait_stats(chunk):
        for flow in (0, 1):

            @pl.when(far_receives[flow])
            def _(flow=flow):
                at = (flow, chunk)
                whole(stat_in.at[at], stat_send.at[flow], stat_recv.at[at], flow).wait_recv()

            @pl.when(receives[flow] & jnp.logical_not(far_receives[flow]))
            def _(flow=flow):
                stat_copy(chunk, flow).wait_recv()

    def dq_copy(chunk, flow, h):
        at = (flow, chunk)
        source, place = (ref.at[flow, chunk, h] for ref in (dq_out, dq_in))
        return remote(source, place, dq_send.at[flow], bulk_recv.at[at], flow)

    def dq_arrival(chunk, flow):
        at = (flow, chunk)
        return whole(dq_in.at[at], dq_send.at[flow], bulk_recv.at[at], flow)

    def start(copies, when=sends):
        for flow in (0, 1):

            @pl.when(when[flow])
            def _(flow=flow):
                for copy in copies(flow):
                    copy.start()

    def wait_send(copies, when=sends):
        for flow in (0, 1):

            @pl.when(when[flow])
            def _(flow=flow):
                for copy in copies(flow):
                    copy.wait_send()

    def wait_recv(copies, when=receives):
        for flow in (0, 1):

            @pl.when(when[flow])
            def _(flow=flow):
                for copy in copies(flow):
                    copy.wait_recv()

    def bulk_copies(chunk):
        return lambda flow: [bulk_copy(chunk, flow, array) for array in (0, 1)]

    start(bulk_copies(jnp.int32(0)))

    for pair in range(PAIRS):
        for array in range(4):
            load(pair, array).start()

    own_copy.wait()
    near_copy.wait()
    lane = lax.broadcasted_iota(jnp.int32, (8, 128), 1)
    low_lane = lax.rem(lane, 64)
    first_id = 8 * (me - 1)
    held = [jnp.full((8, 128), -1, jnp.int32) for _ in range(3)]
    for t in range(24):
        number = first_id + t
        valid = (number >= 0) & (number < 8 * n)
        slot = own_ids[jnp.clip(number, 0, 8 * n - 1)] - first_id
        slot = jnp.where(valid, slot, -1000)
        held = [jnp.where(low_lane == slot - 8 * w, number, held[w]) for w in range(3)]
    near = near_ids[...]
    found = [jnp.zeros((8, 128), jnp.bool_) for _ in range(3)]
    for j in range(16):
        column = jnp.broadcast_to(near[:, j : j + 1], (8, 128))
        found = [found[w] | (column == held[w]) for w in range(3)]
    masks = [jnp.where(found[w] | (low_lane >= 8), 0.0, MASKED) for w in range(3)]
    mask_out[0] = masks[2]
    mask_out[1] = masks[0]
    start(lambda flow: [mask_copy(flow)])
    for chunk in range(1, AHEAD):
        start(bulk_copies(jnp.int32(chunk)))

    def spread(block, mask):
        for a in range(8):
            rows = pl.ds(ROWS * block + 64 * a, 64)
            bias[rows, :] = jnp.broadcast_to(mask[a : a + 1, :], (64, 128)).astype(BF16)

    spread(1, masks[1])
    row_slot = lax.broadcasted_iota(jnp.int32, (ROWS, 128), 0) // 64
    lane_slot = lax.rem(lax.broadcasted_iota(jnp.int32, (ROWS, 128), 1), 64)
    hot[...] = jnp.where(row_slot == lane_slot, 1.0, 0.0).astype(BF16)

    for flow in (0, 1):

        @pl.when(jnp.logical_not(receives[flow]))
        def _(flow=flow):
            rows = pl.ds(2 * ROWS * flow, ROWS)
            for pair in range(PAIRS):
                rows_all[pair, :, rows, :] = jnp.zeros((2, ROWS, 128), BF16)
            mask_in[flow] = jnp.full((8, 128), MASKED, F32)
            stat_in[flow, :, 0:2] = jnp.full((CHUNKS, 2, 8, 128), MASKED, F32)
            dq_in[flow] = jnp.zeros((CHUNKS, 2, 64, TILE), BF16)

        @pl.when(jnp.logical_not(far_receives[flow]))
        def _(flow=flow):
            stat_in[flow, :, 2] = jnp.full((CHUNKS, 8, 128), MASKED, F32)

    middle = pl.ds(ROWS, ROWS)
    places = (k_pair, v_pair, rows_all.at[:, 0, middle], rows_all.at[:, 1, middle])
    for array, place in enumerate(places):
        pltpu.make_async_copy(place, place, load_sem.at[array]).wait()
    for pair in range(PAIRS):
        k_turned[pair] = k_pair[pair].T

    half = lax.broadcasted_iota(jnp.int32, (1, 128), 1) < 64
    halves = (half, jnp.logical_not(half))

    def keys_of(pair, h):
        return (
            jnp.where(halves[h], k_pair[pair], hot[...]),
            jnp.where(halves[h], v_pair[pair], jnp.zeros((), BF16)),
        )

    def scores_of(keys, values, pair, rows, h, e_ref, d_ref):
        queries = jnp.where(halves[h], rows_all[pair, 0, rows, :], bias[rows, :])
        scores = dot_last(keys, queries)
        peak = jnp.max(scores, axis=0, keepdims=True)
        raised = jnp.exp2((scores - peak) * base2)
        e_ref[...] = raised
        dweights = dot_last(values, rows_all[pair, 1, rows, :])
        d_ref[...] = dweights
        total = jnp.sum(raised, axis=0, keepdims=True)
        weighted = jnp.sum(raised * dweights, axis=0, keepdims=True)
        raised_by = peak * base2
        return raised_by, raised_by + jnp.log2(total), weighted / total

    def packed(found):
        rows = [row for peak, log_total, delta in found for row in halved(log_total)]
        rows += [row for peak, log_total, delta in found for row in halved(delta)]
        return jnp.concatenate(rows, axis=0)

    def halved(row):
        return [row[:, :128], row[:, 128:]]

    def keep_peaks(block, chunk, found):
        for h in (0, 1):
            peaks[block, chunk, h : h + 1, :] = found[h][0]

    def own_scores(pair, carry):
        both = [keys_of(pair, h) for h in (0, 1)]
        for t in (0, 1):
            chunk = 2 * pair + t
            found = []
            for h in (0, 1):
                rows = pl.ds(ROWS + TILE * t, TILE)
                found += [
                    scores_of(*both[h], pair, rows, h, e_own.at[chunk, h], d_own.at[chunk, h])
                ]
            keep_peaks(1, chunk, found)
            stat_out[0, chunk, 0] = packed(found)
            stat_out[1, chunk, 0] = packed(found)
        return carry

    lax.fori_loop(0, PAIRS, own_scores, 0)

    wait_recv(lambda flow: [mask_copy(flow)])
    spread(0, mask_in[0])
    spread(2, mask_in[1])

    def near_scores(chunk):
        pair, first = split(chunk)
        slot = lax.rem(chunk, RING)
        found = [[], []]
        for h in (0, 1):
            keys, values = keys_of(pair, h)
            for side in (0, 1):
                rows = pl.ds(2 * ROWS * side + first, TILE)
                e_ref, d_ref = e_near.at[slot, side, h], d_near.at[slot, side, h]
                found[side] += [scores_of(keys, values, pair, rows, h, e_ref, d_ref)]
        for side in (0, 1):
            keep_peaks(2 * side, chunk, found[side])
            stat_out[1 - side, chunk, 1] = packed(found[side])

    def combined(parts):
        logs, deltas = [part[:4] for part in parts], [part[4:] for part in parts]
        top = functools.reduce(jnp.maximum, logs)
        scales = [jnp.exp2(one - top) for one in logs]
        total = sum(scales)
        delta = sum(scale * one for scale, one in zip(scales, deltas)) / total
        return top + jnp.log2(total), delta

    def finish(chunk):
        pair, first = split(chunk)
        slot = lax.rem(chunk, RING)
        finals = [
            combined([stat_out[1, chunk, 1], stat_in[0, chunk, 0], stat_in[0, chunk, 2]]),
            combined([stat_out[0, chunk, 0], stat_in[0, chunk, 1], stat_in[1, chunk, 1]]),
            combined([stat_out[0, chunk, 1], stat_in[1, chunk, 0], stat_in[1, chunk, 2]]),
        ]

        def one(h, block):
            side = block // 2
            if block == 1:
                e_ref, d_ref = e_own.at[chunk, h], d_own.at[chunk, h]
            else:
                e_ref, d_ref = e_near.at[slot, side, h], d_near.at[slot, side, h]
            log_total, delta = (
                jnp.concatenate([one[2 * h : 2 * h + 1], one[2 * h + 1 : 2 * h + 2]], axis=1)
                for one in finals[block]
            )
            weight = e_ref[...] * jnp.exp2(peaks[block, chunk, h : h + 1, :] - log_total)
            dscore = (weight * (d_ref[...] - delta)).astype(BF16)
            lanes = pl.ds(ROWS * block + first, TILE)
            rows = pl.ds(ROWS * h, ROWS)
            weights[rows, lanes] = weight.astype(BF16)
            dscores[rows, lanes] = dscore
            part = dot(k_turned[pair, pl.ds(64 * h, 64), :], dscore)
            if block == 1:
                dq_own[chunk, pl.ds(64 * h, 64), :] = part
            else:
                dq_out[1 - side, chunk, h] = part.astype(BF16)

        for h in (0, 1):
            one(h, 0)
            one(h, 2)

            @pl.when(chunk >= 1)
            def _(h=h):
                start(lambda flow: [dq_copy(chunk, flow, h)])

        @pl.when(chunk == 1)
        def _():
            start(lambda flow: [dq_copy(0, flow, h) for h in (0, 1)])

        for h in (0, 1):
            one(h, 1)

    def key_gradients(pair):
        dv = dot(weights[...], rows_all[pair, 1])
        dk = dot(dscores[...], rows_all[pair, 0])
        lanes = pl.ds(pl.multiple_of(pair * 128, 128), 128)
        grad_value[:, lanes] = jnp.where(half, dv[:ROWS], dv[ROWS:]).astype(BF16)
        grad_key[:, lanes] = (jnp.where(half, dk[:ROWS], dk[ROWS:]) * scaling).astype(BF16)

    def query_gradients(chunk):
        near = [dq_in[flow, chunk].reshape(128, TILE).astype(F32) for flow in (0, 1)]
        total = dq_own[chunk] + near[0] + near[1]
        pair, first = split(chunk)
        lanes = pl.ds(pl.multiple_of(pair * 128, 128), 128)
        grad_query[pl.ds(first, TILE), lanes] = (total * scaling).T.astype(BF16)

    def step(s, carry):
        @pl.when(s < CHUNKS)
        def _():
            wait_recv(lambda flow: [bulk_arrival(s, flow)])
            near_scores(s)
            start(lambda flow: [stat_copy(s, flow)])
            start(lambda flow: [far_copy(s, flow)], far_sends)

            @pl.when(s + AHEAD < CHUNKS - 1)
            def _():
                start(bulk_copies(s + AHEAD))

            @pl.when(s + AHEAD == CHUNKS - 2)
            def _():
                start(bulk_copies(CHUNKS - 1))

        @pl.when((s >= LAG_C) & (s < CHUNKS + LAG_C))
        def _():
            chunk = s - LAG_C
            wait_stats(chunk)
            finish(chunk)

            @pl.when(lax.rem(chunk, 2) == 1)
            def _():
                key_gradients(lax.div(chunk, 2))

        @pl.when(s >= LAG_D)
        def _():
            sum_queries(s - LAG_D)

        return carry

    def sum_queries(chunk):
        wait_recv(lambda flow: [dq_arrival(chunk, flow)])
        query_gradients(chunk)

    lax.fori_loop(0, CHUNKS + LAG_D - 1, step, 0)

    wait_send(
        lambda flow: [
            mask_copy(flow),
            whole(rows_all.at[:, :, middle], bulk_send.at[flow], bulk_recv.at[flow, 0], flow),
            whole(stat_out.at[flow], stat_send.at[flow], stat_recv.at[flow, 0], flow),
            whole(dq_out.at[flow], dq_send.at[flow], bulk_recv.at[flow, 0], flow),
        ]
    )
    wait_send(
        lambda flow: [
            whole(stat_out.at[flow, :, 1], far_send.at[flow], stat_recv.at[flow, 0], flow)
        ],
        far_sends,
    )
    sum_queries(CHUNKS - 1)


def write_out(*refs):
    sources, places, sem = refs[:3], refs[3:6], refs[6]
    copies = [
        pltpu.make_async_copy(source, place, sem.at[i])
        for i, (source, place) in enumerate(zip(sources, places))
    ]
    for copy in copies:
        copy.start()
    for copy in copies:
        copy.wait()


def body(n, query_rows, key_rows, value_rows, grad_output, neighbours, owner):
    rows, features = query_rows.shape
    out = jax.ShapeDtypeStruct((rows, features), BF16)
    far, near = pl.BlockSpec(memory_space=pl.ANY), pl.BlockSpec(memory_space=pltpu.VMEM)
    dma = pltpu.SemaphoreType.DMA
    wide = ROWS * 3
    parts = pl.pallas_call(
        functools.partial(kernel, n),
        out_shape=[pltpu.VMEM((rows, features), BF16)] * 3,
        in_specs=[far] * 6,
        out_specs=[near] * 3,
        scratch_shapes=[
            pltpu.SMEM(owner.shape, jnp.int32),
            pltpu.VMEM(neighbours.shape, jnp.int32),
            pltpu.VMEM((PAIRS, ROWS, 128), BF16),
            pltpu.VMEM((PAIRS, ROWS, 128), BF16),
            pltpu.VMEM((PAIRS, 128, ROWS), BF16),
            pltpu.VMEM((PAIRS, 2, wide, 128), BF16),
            pltpu.VMEM((wide, 128), BF16),
            pltpu.VMEM((ROWS, 128), BF16),
            pltpu.VMEM((2, 8, 128), F32),
            pltpu.VMEM((2, 8, 128), F32),
            pltpu.VMEM((CHUNKS, 2, ROWS, TILE), F32),
            pltpu.VMEM((CHUNKS, 2, ROWS, TILE), F32),
            pltpu.VMEM((RING, 2, 2, ROWS, TILE), F32),
            pltpu.VMEM((RING, 2, 2, ROWS, TILE), F32),
            pltpu.VMEM((3, CHUNKS, 8, TILE), F32),
            pltpu.VMEM((2, CHUNKS, 2, 8, 128), F32),
            pltpu.VMEM((2, CHUNKS, 3, 8, 128), F32),
            pltpu.VMEM((2 * ROWS, wide), BF16),
            pltpu.VMEM((2 * ROWS, wide), BF16),
            pltpu.VMEM((CHUNKS, 128, TILE), F32),
            pltpu.VMEM((2, CHUNKS, 2, 64, TILE), BF16),
            pltpu.VMEM((2, CHUNKS, 2, 64, TILE), BF16),
            dma((6,)),
            dma((2,)),
            dma((2, CHUNKS)),
            dma((2,)),
            dma((2,)),
            dma((2,)),
            dma((2, CHUNKS)),
            dma((2,)),
            dma((2,)),
        ],
        compiler_params=pltpu.CompilerParams(
            collective_id=0, has_side_effects=True, vmem_limit_bytes=58 << 20
        ),
    )(query_rows, key_rows, value_rows, grad_output, neighbours, owner)
    return pl.pallas_call(
        write_out,
        out_shape=[out] * 3,
        in_specs=[near] * 3,
        out_specs=[far] * 3,
        scratch_shapes=[dma((3,))],
    )(*[pltpu.with_memory_space_constraint(one, pltpu.VMEM) for one in parts])


def solution(mesh):
    split = P(("scene", "patch"), None)
    return jax.shard_map(
        functools.partial(body, mesh.shape["patch"]),
        mesh=mesh,
        in_specs=(split, split, split, split, split, P("scene")),
        out_specs=(split, split, split),
        check_vma=False,
    )
```
